512 devices in a mesh: row: 128 (over x, z, y_hi), ch: 4 (over y_lo, core).
Axes of the slice: x: 4, y: 4 (y_hi: 2, y_lo: 2; y = y_hi * 2 + y_lo), z: 16, core: 2. Of those that a mesh axis runs over, the one named last changes fastest.
Arguments:
- pair_rep: bfloat16 [128, 128, 128], P('ch', 'row'), may hold values from -6 to 6
- residue_mask: int32 [128], replicated, may hold values 0 or 1
- chain_ids: int32 [128], replicated, may hold values from 0 to 3, never falling along the last dimension, each value on 1 to 64 neighbouring positions
- in_gain: float32 [2, 128], replicated, may hold values from 0.5 to 1.5
- in_bias: float32 [2, 128], replicated, may hold values from -3 to 3
- w_proj: bfloat16 [2, 128, 4, 128], P(None, None, None, 'ch'), may hold values from -0.5 to 0.5
- w_gate: bfloat16 [2, 128, 128], P(None, None, 'ch'), may hold values from -0.5 to 0.5
- pair_bias: float32 [2, 128], P(None, 'ch'), may hold values from -4 to 4
- out_gain: float32 [2, 128], P(None, 'ch'), may hold values from 0.5 to 1.5
- out_bias: float32 [2, 128], P(None, 'ch'), may hold values from -3 to 3
- w_out: bfloat16 [2, 128, 128], P(None, 'ch'), may hold values from -0.5 to 0.5
Outputs:
- pair_out: bfloat16 [128, 128, 128], P('ch', 'row')
The draws below stay inside these ranges and needn't reach their ends.
Inputs may be any that keep to these rules, and one draw needn't show every extreme that they name: `chain_ids`: chain numbers never fall along the residues; each chain has 1 to 64 residues.
All inputs are finite; a program needn't handle non-finite values.
Results may differ from the reference program's by a relative error of at most 0.013.
Values may be sent and summed in bfloat16 or wider, within the bound.
No kernel may reach another device: no remote copies, remote signals or barrier semaphores. Data moves between devices by JAX's collectives and lax.ppermute only.
A program may use at most 64 MiB of HBM per device.

```python
import math
import jax
import jax.numpy as jnp
import numpy as np
from jax import lax

C = 128
CH = 128
N = 128


def place_ends(array, own_key, least, largest):
    longest = array.shape.index(max(array.shape))
    spots = []
    for shift in (0, 1):
        where = [jax.random.randint(jax.random.fold_in(own_key, axis), (), 0, length) for axis, length in enumerate(array.shape)]
        where[longest] = (where[longest] + shift) % array.shape[longest]
        spots.append(tuple(where))
    return array.at[spots[0]].set(least).at[spots[1]].set(largest)


def shard_levels(key, shape, cuts, smallest, largest):
    level = 1.0
    for position, shards_of in cuts:
        draws = jax.random.uniform(jax.random.fold_in(jax.random.fold_in(key, 6), position), (shards_of,), jnp.float32, smallest / len(cuts), largest / len(cuts))
        level = level * jnp.repeat(jnp.exp(draws), shape[position] // shards_of).reshape((-1,) + (1,) * (len(shape) - 1 - position))
    return level


def split_up(amount, total, reach, lean):
    weights = [(1 << 20) // math.isqrt(grade ** lean) + 1 for grade in range(2, amount + 1)]
    spare, counts = total - reach - (amount - 1), [1] * (amount - 1)
    while spare > 0:
        movable = [i for i in range(amount - 1) if counts[i] < reach]
        whole, left = sum([weights[i] for i in movable]), spare
        for i in movable:
            addition = min(reach - counts[i], max(1, left * weights[i] // whole), spare)
            counts[i] = counts[i] + addition
            spare = spare - addition
    return np.array([reach] + counts)


def uneven(rng, amount, total, bound, skew):
    if amount == 2:
        one = jax.random.randint(rng, (), max(1, total - bound), min(bound, total - 1) + 1)
        return jnp.stack([one, total - one])
    lengths = jnp.asarray(split_up(amount, total, bound, skew), jnp.int32)
    twos = (amount - 1) // 2
    source_of, receiver = lengths[1:1 + 2 * twos:2], lengths[2:2 + 2 * twos:2]
    slack = jnp.minimum(source_of - 1, bound - receiver)
    passed = jax.random.randint(jax.random.fold_in(rng, 1), (twos,), 0, 1 << 20) % (slack + 1)
    lengths = lengths.at[1:1 + 2 * twos:2].set(source_of - passed).at[2:2 + 2 * twos:2].set(receiver + passed)
    return lengths[jax.random.permutation(jax.random.fold_in(rng, 2), amount)]


def bell_draw(own_key, shape, scale, bound, split=(), held_as=jnp.bfloat16):
    drawn = scale * jax.random.normal(own_key, shape, jnp.float32)
    if split:
        drawn = drawn * shard_levels(own_key, shape, split, -0.22, 0.18)
    return jnp.clip(drawn, -bound, bound).astype(held_as)


def setup_inputs(seed: int = 0) -> dict:
    arg_keys = jax.random.split(jax.random.key(seed), 12)
    return {
        "pair_rep": bell_draw(arg_keys[0], (C, N, N), 1.0, 6.0, ((0, 4), (1, 128))),
        "residue_mask": place_ends((jax.random.randint(arg_keys[1], (N,), 0, 8) < 7).astype(jnp.int32), jax.random.fold_in(arg_keys[1], 1), 0, 1),
        "chain_ids": jnp.searchsorted(jnp.cumsum(uneven(arg_keys[2], 4, N, N // 2, 1)), jnp.arange(N), side="right").astype(jnp.int32),
        "in_gain": jnp.clip(1.0 + 0.1 * jax.random.normal(arg_keys[3], (2, C), jnp.float32), 0.5, 1.5),
        "in_bias": bell_draw(arg_keys[4], (2, C), 0.5, 3.0, (), jnp.float32),
        "w_proj": bell_draw(arg_keys[5], (2, C, 4, CH), C ** -0.5, 0.5, ((3, 4),)),
        "w_gate": bell_draw(arg_keys[6], (2, C, C), C ** -0.5, 0.5, ((2, 4),)),
        "pair_bias": bell_draw(arg_keys[7], (2, C), 1.0, 4.0, ((1, 4),), jnp.float32),
        "out_gain": jnp.clip(1.0 + 0.1 * jax.random.normal(arg_keys[8], (2, CH), jnp.float32), 0.5, 1.5),
        "out_bias": bell_draw(arg_keys[9], (2, CH), 0.5, 3.0, ((1, 4),), jnp.float32),
        "w_out": bell_draw(arg_keys[10], (2, CH, C), CH ** -0.5, 0.5, ((1, 4),)),
    }


epsilon = 1e-05

def channel_norm(values, norm_gain, norm_bias):
    mean_val = lax.optimization_barrier(jnp.mean(values, axis=0))
    variance = lax.optimization_barrier(jnp.mean(values * values, axis=0)) - mean_val * mean_val
    return (values - mean_val) * lax.rsqrt(variance + epsilon) * norm_gain[:, None, None] + norm_bias[:, None, None]

def reference(pair_rep, residue_mask, chain_ids, in_gain, in_bias, w_proj, w_gate, pair_bias, out_gain, out_bias, w_out):
    mask_float = residue_mask.astype(jnp.float32)
    pair_mask = mask_float[:, None] * mask_float[None, :]
    same_chain = (chain_ids[:, None] == chain_ids[None, :]).astype(jnp.float32)

    def update(pair_in, layer, incoming):
        normed = channel_norm(pair_in.astype(jnp.float32), in_gain[layer], in_bias[layer]).astype(jnp.bfloat16)
        normed_f = normed.astype(jnp.float32)
        projected = jnp.einsum('cij,cpd->pdij', normed_f, w_proj[layer].astype(jnp.float32))
        left_arm = (jax.nn.sigmoid(projected[0]) * projected[1] * pair_mask).astype(jnp.bfloat16).astype(jnp.float32)
        right_arm = (jax.nn.sigmoid(projected[2]) * projected[3] * pair_mask).astype(jnp.bfloat16).astype(jnp.float32)
        if incoming:
            product_sum = jnp.einsum('dki,dkj->dij', left_arm, right_arm)
        else:
            product_sum = jnp.einsum('dik,djk->dij', left_arm, right_arm)
        normed_x = channel_norm(product_sum, out_gain[layer], out_bias[layer]).astype(jnp.bfloat16)
        mixed = jnp.einsum('dij,dc->cij', normed_x.astype(jnp.float32), w_out[layer].astype(jnp.float32))
        logits = jnp.einsum('cij,cd->dij', normed_f, w_gate[layer].astype(jnp.float32)) + pair_bias[layer][:, None, None] * same_chain[None]
        return (pair_in.astype(jnp.float32) + jax.nn.sigmoid(logits) * mixed).astype(jnp.bfloat16)
    middle = update(pair_rep, 0, False)
    return update(middle, 1, True)
```

```python
import jax
import jax.numpy as jnp
from jax import lax
from jax.sharding import Mesh, PartitionSpec as P

epsilon = 1e-05
bf16 = jnp.bfloat16
f32 = jnp.float32
ROW = ("x", "z", "yh")
PLANE = ("x", "yh", "ch")


def norm(v, gain, bias):
    mean = jnp.mean(v, axis=0)
    var = jnp.mean(v * v, axis=0) - mean * mean
    return ((v - mean) * lax.rsqrt(var + epsilon) * gain[:, None] + bias[:, None]).astype(bf16)


def body(pair_rep, residue_mask, chain_ids, in_gain, in_bias, w_proj, w_gate, pair_bias, out_gain, out_bias, w_out):
    ix, iz, iyh, q = (lax.axis_index(a) for a in ("x", "z", "yh", "ch"))
    row = (ix * 16 + iz) * 2 + iyh
    me = ix * 8 + iyh * 4 + q
    mask = residue_mask.astype(f32)
    zfull = lax.all_gather(pair_rep[:, 0, :], "ch", axis=0, tiled=True)
    wp1 = lax.all_gather(w_proj[1], "ch", axis=2, tiled=True)
    wg = lax.all_gather(w_gate, "ch", axis=2, tiled=True)
    wo = lax.all_gather(w_out, "ch", axis=0)
    pbias = lax.all_gather(pair_bias, "ch", axis=1, tiled=True)
    og = lax.all_gather(out_gain, "ch", axis=0)
    ob = lax.all_gather(out_bias, "ch", axis=0)

    n0 = norm(zfull.astype(f32), in_gain[0], in_bias[0])
    p0 = jnp.einsum("ck,cpd->pdk", n0, w_proj[0], preferred_element_type=f32)
    pm = mask[row] * mask
    left = (jax.nn.sigmoid(p0[0]) * p0[1] * pm).astype(bf16).reshape(8, 4, 128)
    right = (jax.nn.sigmoid(p0[2]) * p0[3] * pm).astype(bf16).reshape(8, 4, 128)
    zt = lax.dynamic_index_in_dim(zfull.T.reshape(4, 8, 4, 128), q, 2, keepdims=False)
    zt = zt.transpose(1, 0, 2)
    send = jnp.stack([left, right, zt], axis=1).reshape(4, 1, 2, 3, 4, 128)
    send = jnp.broadcast_to(send, (4, 16, 2, 3, 4, 128)).reshape(128, 3, 4, 128)
    got = lax.all_to_all(send, ROW, 0, 0, tiled=True)

    x0 = jnp.einsum("jdk,idk->dji", got[:, 1], got[:, 0], preferred_element_type=f32).astype(bf16)
    x0 = x0.reshape(4, 4, 32, 128).transpose(2, 0, 1, 3).reshape(32, 4, 512)
    x0 = lax.all_to_all(x0, PLANE, 0, 0, tiled=True).reshape(128, 512).astype(f32)

    def reorder(w):
        return w.reshape(4, 8, 4, *w.shape[2:]).swapaxes(0, 1).reshape(128, *w.shape[2:])

    cols = jnp.arange(4) * 32 + me
    same = (chain_ids[cols][:, None] == chain_ids[None, :]).astype(f32).reshape(512)
    pm1 = (mask[cols][:, None] * mask[None, :]).reshape(512)
    xn = norm(x0, reorder(og[:, 0]), reorder(ob[:, 0]))
    y = jnp.einsum("dp,dc->cp", xn, reorder(wo[:, 0]), preferred_element_type=f32)
    zp = got[:, 2].transpose(2, 1, 0).reshape(128, 512).astype(f32)
    nz = norm(zp, in_gain[0], in_bias[0])
    gate = jax.nn.sigmoid(
        jnp.einsum("cp,cd->dp", nz, wg[0], preferred_element_type=f32) + pbias[0][:, None] * same
    )
    z1 = (zp + gate * y).astype(bf16)
    n1 = norm(z1.astype(f32), in_gain[1], in_bias[1])
    p1 = jnp.einsum("cp,cxd->xdp", n1, wp1, preferred_element_type=f32)
    left1 = (jax.nn.sigmoid(p1[0]) * p1[1] * pm1).astype(bf16)
    right1 = (jax.nn.sigmoid(p1[2]) * p1[3] * pm1).astype(bf16)
    gate1 = jax.nn.sigmoid(
        jnp.einsum("cp,cd->dp", n1, wg[1], preferred_element_type=f32) + pbias[1][:, None] * same
    ).astype(bf16)
    zg = jnp.stack([z1, gate1]).reshape(2, 4, 32, 4, 4, 16, 2)
    zg = lax.dynamic_index_in_dim(zg, iz, 5, keepdims=False)
    zg = zg.transpose(4, 5, 1, 0, 3, 2).reshape(32, 4, 64)
    send = jnp.concatenate(
        [left1.reshape(32, 4, 512), right1.reshape(32, 4, 512), zg, jnp.zeros((32, 4, 64), bf16)], axis=2
    )
    got = lax.all_to_all(send, PLANE, 0, 0, tiled=True)
    l1 = lax.dynamic_slice_in_dim(got[:, :, :512], iz * 2, 2, 0).reshape(2, 4, 4, 128)
    r1 = got[:, :, 512:1024].reshape(32, 4, 4, 128)
    x1 = jnp.einsum("ydxk,mdtk->xydtm", l1, r1, preferred_element_type=f32).astype(bf16)
    x1 = jnp.broadcast_to(x1.reshape(8, 1, 4, 128), (8, 4, 4, 128)).reshape(32, 4, 128)
    x1 = lax.all_to_all(x1, PLANE, 0, 0, tiled=True).reshape(128, 128).astype(f32)
    xn = norm(x1, og[:, 1].reshape(128), ob[:, 1].reshape(128))
    wo1 = lax.dynamic_slice_in_dim(wo[:, 1].reshape(128, 128), q * 32, 32, 1)
    y = jnp.einsum("dp,dc->cp", xn, wo1, preferred_element_type=f32)
    zg = got[:, :, 1024:1088].reshape(32, 2, 4, 32).transpose(1, 3, 2, 0).reshape(2, 32, 128).astype(f32)
    return (zg[0] + zg[1] * y).astype(bf16)[:, None, :]


def solution(mesh):
    fine = Mesh(mesh.devices.reshape(4, 16, 2, 4), ("x", "z", "yh", "ch"))
    return jax.shard_map(
        body,
        mesh=fine,
        in_specs=(
            P("ch", ROW, None),
            P(),
            P(),
            P(),
            P(),
            P(None, None, None, "ch"),
            P(None, None, "ch"),
            P(None, "ch"),
            P(None, "ch"),
            P(None, "ch"),
            P(None, "ch", None),
        ),
        out_specs=P("ch", ROW, None),
        check_vma=False,
    )
```

```python
import jax
import jax.numpy as jnp
from jax import lax
from jax.sharding import Mesh, PartitionSpec as P

epsilon = 1e-05
bf16 = jnp.bfloat16
f32 = jnp.float32
ROW = ("x", "z", "yh")
PLANE = ("x", "yh", "ch")


def norm(v, gain, bias):
    mean = jnp.mean(v, axis=0)
    var = jnp.mean(v * v, axis=0) - mean * mean
    return ((v - mean) * lax.rsqrt(var + epsilon) * gain[:, None] + bias[:, None]).astype(bf16)


def body(pair_rep, residue_mask, chain_ids, in_gain, in_bias, w_proj, w_gate, pair_bias, out_gain, out_bias, w_out):
    ix, iz, iyh, q = (lax.axis_index(a) for a in ("x", "z", "yh", "ch"))
    row = (ix * 16 + iz) * 2 + iyh
    me = ix * 8 + iyh * 4 + q
    zfull = lax.all_gather(pair_rep[:, 0, :], "ch", axis=0, tiled=True)
    zfull, residue_mask, chain_ids, in_gain, in_bias = lax.optimization_barrier(
        (zfull, residue_mask, chain_ids, in_gain, in_bias)
    )
    mask = residue_mask.astype(f32)
    n0 = norm(zfull.astype(f32), in_gain[0], in_bias[0])
    p0 = jnp.einsum("ck,cpd->pdk", n0, w_proj[0], preferred_element_type=f32)
    pm = mask[row] * mask
    left = (jax.nn.sigmoid(p0[0]) * p0[1] * pm).astype(bf16).reshape(8, 4, 128)
    right = (jax.nn.sigmoid(p0[2]) * p0[3] * pm).astype(bf16).reshape(8, 4, 128)
    zt = lax.dynamic_index_in_dim(zfull.T.reshape(4, 8, 4, 128), q, 2, keepdims=False)
    zt = zt.transpose(1, 0, 2)
    send = jnp.stack([left, right, zt], axis=1).reshape(4, 1, 2, 3, 4, 128)
    send = jnp.broadcast_to(send, (4, 16, 2, 3, 4, 128)).reshape(128, 3, 4, 128)
    got = lax.all_to_all(send, ROW, 0, 0, tiled=True)

    w_gate2 = w_gate.transpose(1, 0, 2).reshape(2, 64, 64).transpose(1, 0, 2).reshape(64, 128)
    packed = jnp.concatenate([w_proj[1].reshape(128, 128), w_gate2, w_out.reshape(64, 128)], axis=0)
    packed = lax.all_gather(packed, "ch", axis=0)
    small = lax.all_gather(jnp.concatenate([pair_bias, out_gain, out_bias], axis=0), "ch", axis=0)
    wp1 = packed[:, :128].reshape(4, 128, 4, 32).transpose(1, 2, 0, 3).reshape(128, 4, 128)
    wg = packed[:, 128:192].reshape(4, 64, 2, 2, 32).transpose(3, 2, 1, 0, 4).reshape(2, 128, 128)
    wo = packed[:, 192:].reshape(4, 2, 32, 128)
    pbias = small[:, 0:2].transpose(1, 0, 2).reshape(2, 128)
    og, ob = small[:, 2:4], small[:, 4:6]

    x0 = jnp.einsum("jdk,idk->dji", got[:, 1], got[:, 0], preferred_element_type=f32).astype(bf16)
    x0 = x0.reshape(4, 4, 32, 128).transpose(2, 0, 1, 3).reshape(32, 4, 512)
    x0 = lax.all_to_all(x0, PLANE, 0, 0, tiled=True).reshape(128, 512).astype(f32)

    def reorder(w):
        return w.reshape(4, 8, 4, *w.shape[2:]).swapaxes(0, 1).reshape(128, *w.shape[2:])

    cols = jnp.arange(4) * 32 + me
    same = (chain_ids[cols][:, None] == chain_ids[None, :]).astype(f32).reshape(512)
    pm1 = (mask[cols][:, None] * mask[None, :]).reshape(512)
    xn = norm(x0, reorder(og[:, 0]), reorder(ob[:, 0]))
    y = jnp.einsum("dp,dc->cp", xn, reorder(wo[:, 0]), preferred_element_type=f32)
    zp = got[:, 2].transpose(2, 1, 0).reshape(128, 512).astype(f32)
    nz = norm(zp, in_gain[0], in_bias[0])
    gate = jax.nn.sigmoid(
        jnp.einsum("cp,cd->dp", nz, wg[0], preferred_element_type=f32) + pbias[0][:, None] * same
    )
    z1 = (zp + gate * y).astype(bf16)
    n1 = norm(z1.astype(f32), in_gain[1], in_bias[1])
    p1 = jnp.einsum("cp,cxd->xdp", n1, wp1, preferred_element_type=f32)
    left1 = (jax.nn.sigmoid(p1[0]) * p1[1] * pm1).astype(bf16)
    right1 = (jax.nn.sigmoid(p1[2]) * p1[3] * pm1).astype(bf16)
    gate1 = jax.nn.sigmoid(
        jnp.einsum("cp,cd->dp", n1, wg[1], preferred_element_type=f32) + pbias[1][:, None] * same
    ).astype(bf16)
    zg = jnp.stack([z1, gate1]).reshape(2, 4, 32, 4, 4, 16, 2)
    zg = lax.dynamic_index_in_dim(zg, iz, 5, keepdims=False)
    zg = zg.transpose(4, 5, 1, 0, 3, 2).reshape(32, 4, 64)
    send = jnp.concatenate(
        [left1.reshape(32, 4, 512), right1.reshape(32, 4, 512), zg, jnp.zeros((32, 4, 64), bf16)], axis=2
    )
    got = lax.all_to_all(send, PLANE, 0, 0, tiled=True)
    l1 = lax.dynamic_slice_in_dim(got[:, :, :512], iz * 2, 2, 0).reshape(2, 4, 4, 128)
    r1 = got[:, :, 512:1024].reshape(32, 4, 4, 128)
    x1 = jnp.einsum("ydxk,mdtk->xydtm", l1, r1, preferred_element_type=f32).astype(bf16)
    x1 = jnp.broadcast_to(x1.reshape(8, 1, 4, 128), (8, 4, 4, 128)).reshape(32, 4, 128)
    x1 = lax.all_to_all(x1, PLANE, 0, 0, tiled=True).reshape(128, 128).astype(f32)
    xn = norm(x1, og[:, 1].reshape(128), ob[:, 1].reshape(128))
    wo1 = lax.dynamic_slice_in_dim(wo[:, 1].reshape(128, 128), q * 32, 32, 1)
    y = jnp.einsum("dp,dc->cp", xn, wo1, preferred_element_type=f32)
    zg = got[:, :, 1024:1088].reshape(32, 2, 4, 32).transpose(1, 3, 2, 0).reshape(2, 32, 128).astype(f32)
    return (zg[0] + zg[1] * y).astype(bf16)[:, None, :]


def solution(mesh):
    fine = Mesh(mesh.devices.reshape(4, 16, 2, 4), ("x", "z", "yh", "ch"))
    return jax.shard_map(
        body,
        mesh=fine,
        in_specs=(
            P("ch", ROW, None),
            P(),
            P(),
            P(),
            P(),
            P(None, None, None, "ch"),
            P(None, None, "ch"),
            P(None, "ch"),
            P(None, "ch"),
            P(None, "ch"),
            P(None, "ch", None),
        ),
        out_specs=P("ch", ROW, None),
        check_vma=False,
    )
```

```python
import jax
import jax.numpy as jnp
from jax import lax
from jax.sharding import Mesh, PartitionSpec as P

epsilon = 1e-05
bf16 = jnp.bfloat16
f32 = jnp.float32
ROW = ("x", "z", "yh")
PLANE = ("x", "yh", "ch")


def norm(v, gain, bias):
    mean = jnp.mean(v, axis=0)
    var = jnp.mean(v * v, axis=0) - mean * mean
    return ((v - mean) * lax.rsqrt(var + epsilon) * gain[:, None] + bias[:, None]).astype(bf16)


def three(v):
    hi = lax.reduce_precision(v, 8, 7)
    mid = lax.reduce_precision(v - hi, 8, 7)
    return jnp.stack([hi, mid, v - hi - mid]).astype(bf16)


def by_plane(v):
    return v.reshape(4, 16, 2).swapaxes(1, 2).reshape(128)


def body(pair_rep, residue_mask, chain_ids, in_gain, in_bias, w_proj, w_gate, pair_bias, out_gain, out_bias, w_out):
    ix, iz, iyh, q = (lax.axis_index(a) for a in ("x", "z", "yh", "ch"))
    send = pair_rep.reshape(4, 8, 4, 16, 2).transpose(2, 1, 0, 4, 3).reshape(1, 4, 8, 128)
    send = jnp.broadcast_to(send, (16, 4, 8, 128)).reshape(64, 8, 128)
    got = lax.all_to_all(send, ("z", "ch"), 0, 0, tiled=True)

    packed = jnp.concatenate(
        [
            w_proj.reshape(256, 128),
            w_gate.transpose(1, 0, 2).reshape(64, 128),
            w_out.reshape(64, 128),
            jnp.pad(three(jnp.stack([pair_bias, out_gain, out_bias])).reshape(576), (0, 448)).reshape(8, 128),
        ],
        axis=0,
    )
    packed = lax.all_gather(packed, "ch", axis=0)
    wp = packed[:, :256].reshape(4, 2, 128, 4, 32).transpose(1, 2, 3, 0, 4).reshape(2, 128, 4, 128)
    wg = packed[:, 256:320].reshape(4, 128, 2, 32).transpose(2, 1, 0, 3).reshape(2, 128, 128)
    wo = packed[:, 320:384].reshape(4, 2, 32, 128).swapaxes(0, 1).reshape(2, 128, 128)
    small = packed[:, 384:].reshape(4, 1024)[:, :576].reshape(4, 3, 3, 2, 32).astype(f32)
    small = (small[:, 0] + small[:, 1] + small[:, 2]).transpose(1, 2, 0, 3).reshape(3, 2, 128)
    pbias, og, ob = small[0], small[1], small[2]

    mask = by_plane(residue_mask.astype(f32)).reshape(8, 16)
    chain = by_plane(chain_ids).reshape(8, 16)
    mine = ix * 2 + iyh
    mask_r = lax.dynamic_index_in_dim(mask, mine, 0, keepdims=False)
    chain_r = lax.dynamic_index_in_dim(chain, mine, 0, keepdims=False)
    mask_c = lax.dynamic_index_in_dim(mask.reshape(4, 32), q, 0, keepdims=False)
    chain_c = lax.dynamic_index_in_dim(chain.reshape(4, 32), q, 0, keepdims=False)
    pm = (mask_r[:, None] * mask_c[None, :]).reshape(512)
    same = (chain_r[:, None] == chain_c[None, :]).astype(f32).reshape(512)

    z0 = got.reshape(16, 4, 8, 4, 32).transpose(1, 3, 2, 0, 4).reshape(128, 512).astype(f32)
    n0 = norm(z0, in_gain[0], in_bias[0])
    p0 = jnp.einsum("cp,cxd->xdp", n0, wp[0], preferred_element_type=f32)
    left = (jax.nn.sigmoid(p0[0]) * p0[1] * pm).astype(bf16)
    right = (jax.nn.sigmoid(p0[2]) * p0[3] * pm).astype(bf16)
    send = jnp.stack([left, right]).reshape(2, 4, 32, 16, 32).transpose(2, 0, 3, 1, 4).reshape(32, 32, 128)
    got = lax.all_to_all(send, PLANE, 0, 0, tiled=True).reshape(8, 4, 2, 16, 4, 32)
    x0 = jnp.einsum("aqzdk,bqydk->dazby", got[:, :, 0], got[:, :, 1], preferred_element_type=f32).astype(bf16)
    x0 = x0.reshape(4, 8, 16, 4, 32).transpose(1, 3, 2, 0, 4).reshape(32, 16, 128)
    x0 = lax.all_to_all(x0, PLANE, 0, 0, tiled=True)
    gate = jax.nn.sigmoid(
        jnp.einsum("cp,cd->dp", n0, wg[0], preferred_element_type=f32) + pbias[0][:, None] * same
    )
    x0 = x0.reshape(32, 16, 4, 32).transpose(2, 0, 1, 3).reshape(128, 512).astype(f32)
    xn = norm(x0, og[0], ob[0])
    y = jnp.einsum("dp,dc->cp", xn, wo[0], preferred_element_type=f32)
    z1 = (z0 + gate * y).astype(bf16)
    n1 = norm(z1.astype(f32), in_gain[1], in_bias[1])
    p1 = jnp.einsum("cp,cxd->xdp", n1, wp[1], preferred_element_type=f32)
    left = (jax.nn.sigmoid(p1[0]) * p1[1] * pm).astype(bf16)
    right = (jax.nn.sigmoid(p1[2]) * p1[3] * pm).astype(bf16)
    left = lax.dynamic_index_in_dim(left.reshape(4, 32, 16, 2, 16), iz, 4, keepdims=False)
    left = jnp.pad(left.transpose(1, 2, 0, 3).reshape(32, 16, 8), ((0, 0), (0, 0), (0, 120)))
    right = right.reshape(4, 32, 16, 32).transpose(1, 2, 0, 3).reshape(32, 16, 128)
    got = lax.all_to_all(jnp.concatenate([right, left], axis=1), PLANE, 0, 0, tiled=True)

    z1_row = lax.dynamic_slice_in_dim(z1, iz * 32, 32, 1)
    n1_row = lax.dynamic_slice_in_dim(n1, iz * 32, 32, 1)
    same_row = lax.dynamic_slice_in_dim(same, iz * 32, 32, 0)
    gate1 = jax.nn.sigmoid(
        jnp.einsum("cp,cd->dp", n1_row, wg[1], preferred_element_type=f32) + pbias[1][:, None] * same_row
    ).astype(bf16)
    zg = jnp.stack([z1_row, gate1]).reshape(2, 4, 4, 8, 32).transpose(1, 0, 3, 2, 4).reshape(4, 16, 128)
    zg = lax.all_to_all(zg, "ch", 0, 0, tiled=True)
    zg = zg.reshape(4, 2, 8, 4, 32).transpose(1, 3, 2, 0, 4).reshape(2, 32, 128).astype(f32)

    r1 = got[:, :16].reshape(8, 4, 16, 4, 32)
    l1 = got[:, 16:, :8].reshape(8, 4, 16, 4, 2)
    x1 = jnp.einsum("aqzdy,apzdk->qydpk", l1, r1, preferred_element_type=f32).astype(bf16)
    x1 = jnp.broadcast_to(x1.reshape(8, 1, 4, 128), (8, 4, 4, 128)).reshape(32, 4, 128)
    x1 = lax.all_to_all(x1, PLANE, 0, 0, tiled=True)
    x1 = x1.swapaxes(0, 1).reshape(128, 128).astype(f32)
    xn = norm(x1, og[1], ob[1])
    wo1 = lax.dynamic_slice_in_dim(wo[1], q * 32, 32, 1)
    y = jnp.einsum("dp,dc->cp", xn, wo1, preferred_element_type=f32)
    out = (zg[0] + zg[1] * y).astype(bf16)
    return out.reshape(32, 4, 2, 16).swapaxes(2, 3).reshape(32, 1, 128)


def solution(mesh):
    fine = Mesh(mesh.devices.reshape(4, 16, 2, 4), ("x", "z", "yh", "ch"))
    return jax.shard_map(
        body,
        mesh=fine,
        in_specs=(
            P("ch", ROW, None),
            P(),
            P(),
            P(),
            P(),
            P(None, None, None, "ch"),
            P(None, None, "ch"),
            P(None, "ch"),
            P(None, "ch"),
            P(None, "ch"),
            P(None, "ch", None),
        ),
        out_specs=P("ch", ROW, None),
        check_vma=False,
    )
```

```python
import jax
import jax.numpy as jnp
from jax import lax
from jax.experimental import pallas as pl
from jax.experimental.pallas import tpu as pltpu
from jax.sharding import Mesh, PartitionSpec as P

epsilon = 1e-05
bf16 = jnp.bfloat16
f32 = jnp.float32
ROW = ("x", "z", "yh")
PLANE = ("x", "yh", "ch")
VMEM = pl.BlockSpec(memory_space=pltpu.VMEM)
SMEM = pl.BlockSpec(memory_space=pltpu.SMEM)


def call(kernel, outs, ins, scratch=(), flops=100_000_000):
    specs = [SMEM if a.dtype == jnp.int32 else VMEM for a in ins]
    moved = sum(a.size * a.dtype.itemsize for a in ins)
    return pl.pallas_call(
        kernel,
        out_shape=[jax.ShapeDtypeStruct(s, d) for s, d in outs],
        in_specs=specs,
        out_specs=[VMEM] * len(outs),
        scratch_shapes=[pltpu.VMEM(s, f32) for s in scratch],
        compiler_params=pltpu.CompilerParams(vmem_limit_bytes=32 * 1024 * 1024),
        cost_estimate=pl.CostEstimate(flops=flops, bytes_accessed=moved, transcendentals=0),
    )(*ins)


def tn(a, b):
    return lax.dot_general(a, b, (((0,), (0,)), ((), ())), preferred_element_type=f32)


def nt(a, b):
    return lax.dot_general(a, b, (((1,), (1,)), ((), ())), preferred_element_type=f32)


def sigmoid(v):
    return 1.0 / (1.0 + jnp.exp(-v))


def norm(v, gain, bias):
    mean = jnp.mean(v, axis=0, keepdims=True)
    var = jnp.mean(v * v, axis=0, keepdims=True) - mean * mean
    return ((v - mean) * lax.rsqrt(var + epsilon) * gain + bias).astype(bf16)


def lanes(pieces):
    return jnp.concatenate(pieces, axis=1)


def permutation():
    k = lax.broadcasted_iota(jnp.int32, (128, 128), 0)
    p = lax.broadcasted_iota(jnp.int32, (128, 128), 1)
    place = (k & 96) | ((k & 1) << 4) | ((k & 31) >> 1)
    return (place == p).astype(f32).astype(bf16)


def spread_kernel(x_ref, out_ref):
    t = jnp.dot(x_ref[...], permutation(), preferred_element_type=f32)
    for q in range(4):
        piece = lanes([t[c * 8 : c * 8 + 8, q * 32 : q * 32 + 32] for c in range(4)]).astype(bf16)
        for z in range(16):
            out_ref[z * 4 + q] = piece


def project(n, u, packed_ref, pm, out_ref, scr):
    sides = ([], [])
    for q in range(4):
        p = tn(packed_ref[q, u * 128 : u * 128 + 128, :], n)
        sides[0].append(sigmoid(p[0:32]) * p[32:64] * pm)
        sides[1].append(sigmoid(p[64:96]) * p[96:128] * pm)
    for s in range(2):
        for z in range(16):
            scr[pl.ds(s * 16 + z, 32, stride=32), :] = lanes([v[:, z * 32 : z * 32 + 32] for v in sides[s]])
    out_ref[...] = scr[...].astype(bf16).reshape(32, 32, 128)


def first_kernel(got_ref, cols_ref, packed_ref, pm_ref, out_ref, z_ref, n_ref, scr):
    rows = []
    for q in range(4):
        for c in range(4):
            pieces = [got_ref[z * 4 + q].astype(f32)[:, c * 32 : c * 32 + 32] for z in range(16)]
            rows.append(lanes(pieces))
    z0 = jnp.concatenate(rows, axis=0)
    z_ref[...] = z0
    n = norm(z0, cols_ref[:, 0:1], cols_ref[:, 2:3])
    n_ref[...] = n
    project(n, 0, packed_ref, pm_ref[...], out_ref, scr)


def gate_kernel(n_ref, packed_ref, cols_ref, same_ref, out_ref):
    for q in range(4):
        w = packed_ref[q, 256:384, 0:32]
        logits = tn(w, n_ref[...])
        out_ref[q * 32 : q * 32 + 32, :] = sigmoid(
            logits + cols_ref[q * 32 : q * 32 + 32, 8:9] * same_ref[...]
        )


def outgoing_kernel(got_ref, out_ref):
    row = lax.broadcasted_iota(jnp.int32, (128, 512), 0) >> 5
    lane = (lax.broadcasted_iota(jnp.int32, (128, 512), 1) >> 5) & 3
    same = row == lane
    left, right = [], []
    for q in range(4):
        left.append(jnp.concatenate([got_ref[a * 4 + q, 0:16, :] for a in range(8)], axis=0))
        right.append(jnp.concatenate([got_ref[a * 4 + q, 16:32, :] for a in range(8)], axis=0))
    left, right = lanes(left), lanes(right)
    for q in range(4):
        part = right[q * 32 : q * 32 + 32].astype(f32)
        block = jnp.where(same, jnp.concatenate([part] * 4, axis=0), 0.0).astype(bf16)
        x = nt(left, block).astype(bf16)
        for b in range(8):
            out_ref[b * 4 + q] = x[b * 16 : b * 16 + 16]


def middle_kernel(got_ref, z_ref, gate_ref, cols_ref, packed_ref, pm_ref, out_ref, z1_ref, n1_ref, scr, xs):
    xs[...] = got_ref[...].astype(f32).reshape(512, 128)
    slabs = [xs[pl.ds(z, 32, stride=16), :] for z in range(16)]
    x0 = jnp.concatenate(
        [lanes([s[:, d * 32 : d * 32 + 32] for s in slabs]) for d in range(4)], axis=0
    )
    xn = norm(x0, cols_ref[:, 4:5], cols_ref[:, 6:7])
    w = jnp.concatenate([packed_ref[q, 384:416, :] for q in range(4)], axis=0)
    z1 = (z_ref[...] + gate_ref[...] * tn(w, xn)).astype(bf16)
    z1_ref[...] = z1
    n1 = norm(z1.astype(f32), cols_ref[:, 1:2], cols_ref[:, 3:4])
    n1_ref[...] = n1
    project(n1, 1, packed_ref, pm_ref[...], out_ref, scr)


def own_kernel(at_ref, z1_ref, n1_ref, packed_ref, cols_ref, same_ref, out_ref):
    lane = lax.broadcasted_iota(jnp.int32, (512, 128), 0)
    col = lax.broadcasted_iota(jnp.int32, (512, 128), 1)
    pick = ((lane == at_ref[0] * 32 + col) & (col < 32)).astype(f32).astype(bf16)
    z1 = jnp.dot(z1_ref[...], pick, preferred_element_type=f32)
    n1 = jnp.dot(n1_ref[...], pick, preferred_element_type=f32).astype(bf16)
    same = jnp.dot(
        jnp.broadcast_to(same_ref[...], (8, 512)).astype(bf16), pick, preferred_element_type=f32
    )[0:1]
    for q in range(4):
        w = packed_ref[q, 256:384, 32:64]
        gate = sigmoid(tn(w, n1) + cols_ref[q * 32 : q * 32 + 32, 9:10] * same)
        part = z1[q * 32 : q * 32 + 32]
        out_ref[q * 32 : q * 32 + 32, :] = lanes(
            [part[:, 0:32], gate[:, 0:32], jnp.zeros((32, 64), f32)]
        ).astype(bf16)


def incoming_kernel(at_ref, got_ref, out_ref, scr):
    left, right = [], []
    for q in range(4):
        left.append(jnp.concatenate([got_ref[a * 4 + q, 0:16, :] for a in range(8)], axis=0))
        right.append(jnp.concatenate([got_ref[a * 4 + q, 16:32, :] for a in range(8)], axis=0))
    row = lax.broadcasted_iota(jnp.int32, (32, 512), 0)
    lane = lax.broadcasted_iota(jnp.int32, (32, 512), 1)
    want = (((row >> 1) & 3) << 7) | ((row >> 3) << 5) | ((row & 1) << 4) | at_ref[0]
    pick = (lane == want).astype(f32).astype(bf16)
    mine = nt(pick, lanes(left)).astype(bf16)
    prods = [jnp.dot(mine, r, preferred_element_type=f32) for r in right]
    for d in range(4):
        x = lanes([p[d * 8 : d * 8 + 8, d * 32 : d * 32 + 32] for p in prods])
        for q in range(4):
            scr[pl.ds(q * 8 + d, 8, stride=32), :] = x
            scr[pl.ds(q * 8 + d + 4, 8, stride=32), :] = x
    out_ref[...] = scr[...].astype(bf16).reshape(32, 8, 128)


def last_kernel(at_ref, got_ref, zg_ref, packed_ref, cols_ref, out_ref, xs, ys):
    xs[...] = got_ref[...].astype(f32).reshape(256, 128)
    x1 = jnp.concatenate([xs[pl.ds(d, 32, stride=8), :] for d in range(4)], axis=0)
    xn = norm(x1, cols_ref[:, 5:6], cols_ref[:, 7:8])
    w = jnp.concatenate([packed_ref[q, 416:448, :] for q in range(4)], axis=0)
    ys[...] = tn(w, xn)
    start = pl.multiple_of(at_ref[1] * 32, 32)
    y = ys[pl.ds(start, 32), :]
    parts = [zg_ref[s, pl.ds(start, 32), :].astype(f32) for s in range(4)]
    z1 = lanes([p[:, 0:32] for p in parts])
    gate = lanes([p[:, 32:64] for p in parts])
    out = (z1 + gate * y).astype(bf16)
    out_ref[...] = nt(out, permutation()).astype(bf16)


def three(v):
    hi = lax.reduce_precision(v, 8, 7)
    mid = lax.reduce_precision(v - hi, 8, 7)
    return jnp.stack([hi, mid, v - hi - mid]).astype(bf16)


def by_plane(v):
    return v.reshape(4, 16, 2).swapaxes(1, 2).reshape(128)


def body(pair_rep, residue_mask, chain_ids, in_gain, in_bias, w_proj, w_gate, pair_bias, out_gain, out_bias, w_out):
    ix, iz, iyh, q = (lax.axis_index(a) for a in ("x", "z", "yh", "ch"))
    at = jnp.stack([iz, q]).astype(jnp.int32)
    (send,) = call(spread_kernel, [((64, 8, 128), bf16)], [pair_rep.reshape(32, 128)])
    got = lax.all_to_all(send, ("z", "ch"), 0, 0, tiled=True)

    gates = jnp.concatenate([w_gate[0], w_gate[1], jnp.zeros((128, 64), bf16)], axis=1)
    small = three(jnp.stack([out_gain, out_bias, pair_bias])).reshape(18, 32)
    packed = jnp.concatenate(
        [w_proj.reshape(256, 128), gates, w_out.reshape(64, 128), jnp.pad(small, ((0, 14), (0, 96)))], axis=0
    )
    packed = lax.all_gather(packed, "ch", axis=0)
    small = packed[:, 448:466, :32].reshape(4, 3, 6, 32).astype(f32).sum(axis=1)
    small = small.transpose(0, 2, 1).reshape(128, 6)
    cols = jnp.concatenate([in_gain.T, in_bias.T, small], axis=1)

    mask = by_plane(residue_mask.astype(f32)).reshape(8, 16)
    chain = by_plane(chain_ids).reshape(8, 16)
    mine = ix * 2 + iyh
    mask_r = lax.dynamic_index_in_dim(mask, mine, 0, keepdims=False)
    chain_r = lax.dynamic_index_in_dim(chain, mine, 0, keepdims=False)
    mask_c = lax.dynamic_index_in_dim(mask.reshape(4, 32), q, 0, keepdims=False)
    chain_c = lax.dynamic_index_in_dim(chain.reshape(4, 32), q, 0, keepdims=False)
    pm = (mask_r[:, None] * mask_c[None, :]).reshape(1, 512)
    same = (chain_r[:, None] == chain_c[None, :]).astype(f32).reshape(1, 512)

    send, z0, n0 = call(
        first_kernel,
        [((32, 32, 128), bf16), ((128, 512), f32), ((128, 512), bf16)],
        [got, cols, packed, pm],
        [(1024, 128)],
    )
    got = lax.all_to_all(send, PLANE, 0, 0, tiled=True)
    (gate,) = call(gate_kernel, [((128, 512), f32)], [n0, packed, cols, same])
    (send,) = call(outgoing_kernel, [((32, 16, 128), bf16)], [got])
    got = lax.all_to_all(send, PLANE, 0, 0, tiled=True)
    send, z1, n1 = call(
        middle_kernel,
        [((32, 32, 128), bf16), ((128, 512), bf16), ((128, 512), bf16)],
        [got, z0, gate, cols, packed, pm],
        [(1024, 128), (512, 128)],
    )
    got = lax.all_to_all(send, PLANE, 0, 0, tiled=True)
    (zg,) = call(own_kernel, [((128, 128), bf16)], [at, z1, n1, packed, cols, same])
    (send,) = call(incoming_kernel, [((32, 8, 128), bf16)], [at, got], [(256, 128)])
    send, zg = lax.optimization_barrier((send, zg))
    got = lax.all_to_all(send, PLANE, 0, 0, tiled=True)
    zg = lax.all_gather(zg, "ch", axis=0)
    (out,) = call(
        last_kernel, [((32, 128), bf16)], [at, got, zg, packed, cols], [(256, 128), (128, 128)]
    )
    return out.reshape(32, 1, 128)


def solution(mesh):
    fine = Mesh(mesh.devices.reshape(4, 16, 2, 4), ("x", "z", "yh", "ch"))
    return jax.shard_map(
        body,
        mesh=fine,
        in_specs=(
            P("ch", ROW, None),
            P(),
            P(),
            P(),
            P(),
            P(None, None, None, "ch"),
            P(None, None, "ch"),
            P(None, "ch"),
            P(None, "ch"),
            P(None, "ch"),
            P(None, "ch", None),
        ),
        out_specs=P("ch", ROW, None),
        check_vma=False,
    )
```

```python
import jax
import jax.numpy as jnp
from jax import lax
from jax.experimental import pallas as pl
from jax.experimental.pallas import tpu as pltpu
from jax.sharding import Mesh, PartitionSpec as P

epsilon = 1e-05
bf16 = jnp.bfloat16
f32 = jnp.float32
ROW = ("x", "z", "yh")
PLANE = ("x", "yh", "ch")
VMEM = pl.BlockSpec(memory_space=pltpu.VMEM)
HBM = pl.BlockSpec(memory_space=pltpu.HBM)


def call(kernel, outs, ins, scratch=(), flops=100_000_000):
    moved = sum(a.size * a.dtype.itemsize for a in ins)
    return pl.pallas_call(
        kernel,
        out_shape=[jax.ShapeDtypeStruct(s, d) for s, d in outs],
        in_specs=[VMEM] * len(ins),
        out_specs=[VMEM] * len(outs),
        scratch_shapes=[pltpu.VMEM(s, f32) for s in scratch],
        compiler_params=pltpu.CompilerParams(vmem_limit_bytes=32 * 1024 * 1024),
        cost_estimate=pl.CostEstimate(flops=flops, bytes_accessed=moved, transcendentals=0),
    )(*ins)


def tn(a, b):
    return lax.dot_general(a, b, (((0,), (0,)), ((), ())), preferred_element_type=f32)


def nt(a, b):
    return lax.dot_general(a, b, (((1,), (1,)), ((), ())), preferred_element_type=f32)


def sigmoid(v):
    return 0.5 * jnp.tanh(0.5 * v) + 0.5


def norm(v, gain, bias):
    mean = jnp.mean(v, axis=0, keepdims=True)
    var = jnp.mean(v * v, axis=0, keepdims=True) - mean * mean
    return ((v - mean) * lax.rsqrt(var + epsilon) * gain + bias).astype(bf16)


def lanes(pieces):
    return jnp.concatenate(pieces, axis=1)


def permutation():
    k = lax.broadcasted_iota(jnp.int32, (128, 128), 0)
    p = lax.broadcasted_iota(jnp.int32, (128, 128), 1)
    place = (k & 96) | ((k & 1) << 4) | ((k & 31) >> 1)
    return (place == p).astype(f32).astype(bf16)


def spread_kernel(x_ref, out_ref, x_vmem, tile, sem_in, sems):
    load = pltpu.make_async_copy(x_ref, x_vmem, sem_in)
    load.start()
    perm = permutation()
    load.wait()
    t = jnp.dot(x_vmem[...], perm, preferred_element_type=f32)
    for q in range(4):
        piece = lanes([t[c * 8 : c * 8 + 8, q * 32 : q * 32 + 32] for c in range(4)])
        tile[q] = piece.astype(bf16)
    copies = [pltpu.make_async_copy(tile, out_ref.at[z * 4 : z * 4 + 4], sems.at[z]) for z in range(16)]
    for c in copies:
        c.start()
    for c in copies:
        c.wait()


def spread(x):
    return pl.pallas_call(
        spread_kernel,
        out_shape=jax.ShapeDtypeStruct((64, 8, 128), bf16),
        in_specs=[HBM],
        out_specs=HBM,
        scratch_shapes=[
            pltpu.VMEM((32, 128), bf16),
            pltpu.VMEM((4, 8, 128), bf16),
            pltpu.SemaphoreType.DMA,
            pltpu.SemaphoreType.DMA((16,)),
        ],
    )(x)


def project(n, w_ref, pm, out_ref, scr):
    sides = ([], [])
    for q in range(4):
        p = jnp.dot(w_ref[q, 0:128, :], n, preferred_element_type=f32)
        sides[0].append(sigmoid(p[0:32]) * p[32:64] * pm)
        sides[1].append(sigmoid(p[64:96]) * p[96:128] * pm)
    for s in range(2):
        for z in range(16):
            scr[pl.ds(s * 16 + z, 32, stride=32), :] = lanes([v[:, z * 32 : z * 32 + 32] for v in sides[s]])
    out_ref[...] = scr[...].astype(bf16).reshape(32, 32, 128)


def first_kernel(got_ref, gain_ref, w_ref, pm_ref, out_ref, z_ref, n_ref, scr):
    rows = []
    for q in range(4):
        for c in range(4):
            pieces = [got_ref[z * 4 + q].astype(f32)[:, c * 32 : c * 32 + 32] for z in range(16)]
            rows.append(lanes(pieces))
    z0 = jnp.concatenate(rows, axis=0)
    z_ref[...] = z0
    n = norm(z0, gain_ref[:, 0:1], gain_ref[:, 2:3])
    n_ref[...] = n
    project(n, w_ref, pm_ref[...], out_ref, scr)


def gate_kernel(n_ref, packed_ref, cols_ref, same_ref, out_ref):
    for q in range(4):
        logits = jnp.dot(packed_ref[q, 128:160, :], n_ref[...], preferred_element_type=f32)
        out_ref[q * 32 : q * 32 + 32, :] = sigmoid(
            logits + cols_ref[q * 32 : q * 32 + 32, 4:5] * same_ref[...]
        )


def outgoing_kernel(got_ref, out_ref):
    row = lax.broadcasted_iota(jnp.int32, (128, 512), 0) >> 5
    lane = (lax.broadcasted_iota(jnp.int32, (128, 512), 1) >> 5) & 3
    same = row == lane
    left, right = [], []
    for q in range(4):
        left.append(jnp.concatenate([got_ref[a * 4 + q, 0:16, :] for a in range(8)], axis=0))
        right.append(jnp.concatenate([got_ref[a * 4 + q, 16:32, :] for a in range(8)], axis=0))
    left, right = lanes(left), lanes(right)
    for q in range(4):
        part = right[q * 32 : q * 32 + 32].astype(f32)
        block = jnp.where(same, jnp.concatenate([part] * 4, axis=0), 0.0).astype(bf16)
        x = nt(left, block).astype(bf16)
        for b in range(8):
            out_ref[b * 4 + q] = x[b * 16 : b * 16 + 16]


def middle_kernel(got_ref, z_ref, gate_ref, gain_ref, cols_ref, packed_ref, pm_ref, out_ref, z1_ref, n1_ref, scr, xs):
    xs[...] = got_ref[...].astype(f32).reshape(512, 128)
    slabs = [xs[pl.ds(z, 32, stride=16), :] for z in range(16)]
    x0 = jnp.concatenate(
        [lanes([s[:, d * 32 : d * 32 + 32] for s in slabs]) for d in range(4)], axis=0
    )
    xn = norm(x0, cols_ref[:, 0:1], cols_ref[:, 2:3])
    w = jnp.concatenate([packed_ref[q, 192:224, :] for q in range(4)], axis=0)
    z1 = (z_ref[...] + gate_ref[...] * tn(w, xn)).astype(bf16)
    z1_ref[...] = z1
    n1 = norm(z1.astype(f32), gain_ref[:, 1:2], gain_ref[:, 3:4])
    n1_ref[...] = n1
    project(n1, packed_ref, pm_ref[...], out_ref, scr)


def own_kernel(z1_ref, n1_ref, packed_ref, cols_ref, same_ref, out_ref):
    lane = lax.broadcasted_iota(jnp.int32, (512, 128), 0)
    col = lax.broadcasted_iota(jnp.int32, (512, 128), 1)
    pick = ((lane == lax.axis_index("z") * 32 + col) & (col < 32)).astype(f32).astype(bf16)
    z1 = jnp.dot(z1_ref[...], pick, preferred_element_type=f32)
    n1 = jnp.dot(n1_ref[...], pick, preferred_element_type=f32).astype(bf16)
    same = jnp.dot(
        jnp.broadcast_to(same_ref[...], (8, 512)).astype(bf16), pick, preferred_element_type=f32
    )[0:1]
    for q in range(4):
        logits = jnp.dot(packed_ref[q, 160:192, :], n1, preferred_element_type=f32)
        gate = sigmoid(logits + cols_ref[q * 32 : q * 32 + 32, 5:6] * same)
        part = z1[q * 32 : q * 32 + 32]
        out_ref[q * 32 : q * 32 + 32, :] = lanes(
            [part[:, 0:32], gate[:, 0:32], jnp.zeros((32, 64), f32)]
        ).astype(bf16)


def incoming_kernel(got_ref, out_ref, scr):
    left, right = [], []
    for q in range(4):
        left.append(jnp.concatenate([got_ref[a * 4 + q, 0:16, :] for a in range(8)], axis=0))
        right.append(jnp.concatenate([got_ref[a * 4 + q, 16:32, :] for a in range(8)], axis=0))
    row = lax.broadcasted_iota(jnp.int32, (32, 512), 0)
    lane = lax.broadcasted_iota(jnp.int32, (32, 512), 1)
    want = (((row >> 1) & 3) << 7) | ((row >> 3) << 5) | ((row & 1) << 4) | lax.axis_index("z")
    pick = (lane == want).astype(f32).astype(bf16)
    mine = nt(pick, lanes(left)).astype(bf16)
    prods = [jnp.dot(mine, r, preferred_element_type=f32) for r in right]
    for d in range(4):
        x = lanes([p[d * 8 : d * 8 + 8, d * 32 : d * 32 + 32] for p in prods])
        for q in range(4):
            scr[pl.ds(q * 8 + d, 8, stride=32), :] = x
            scr[pl.ds(q * 8 + d + 4, 8, stride=32), :] = x
    out_ref[...] = scr[...].astype(bf16).reshape(32, 8, 128)


def last_kernel(got_ref, zg_ref, packed_ref, cols_ref, out_ref, xs, ys):
    xs[...] = got_ref[...].astype(f32).reshape(256, 128)
    x1 = jnp.concatenate([xs[pl.ds(d, 32, stride=8), :] for d in range(4)], axis=0)
    xn = norm(x1, cols_ref[:, 1:2], cols_ref[:, 3:4])
    w = jnp.concatenate([packed_ref[q, 224:256, :] for q in range(4)], axis=0)
    ys[...] = tn(w, xn)
    start = pl.multiple_of(lax.axis_index("ch") * 32, 32)
    y = ys[pl.ds(start, 32), :]
    parts = [zg_ref[s, pl.ds(start, 32), :].astype(f32) for s in range(4)]
    z1 = lanes([p[:, 0:32] for p in parts])
    gate = lanes([p[:, 32:64] for p in parts])
    out = (z1 + gate * y).astype(bf16)
    out_ref[...] = nt(out, permutation()).astype(bf16)


def three(v):
    hi = lax.reduce_precision(v, 8, 7)
    mid = lax.reduce_precision(v - hi, 8, 7)
    return jnp.stack([hi, mid, v - hi - mid]).astype(bf16)


def by_plane(v):
    return v.reshape(4, 16, 2).swapaxes(1, 2).reshape(128)


def body(pair_rep, residue_mask, chain_ids, in_gain, in_bias, w_proj, w_gate, pair_bias, out_gain, out_bias, w_out):
    ix, iyh, q = (lax.axis_index(a) for a in ("x", "yh", "ch"))
    send = spread(pair_rep.reshape(32, 128))
    got = lax.all_to_all(send, ("z", "ch"), 0, 0, tiled=True)

    w_proj = w_proj.transpose(0, 2, 3, 1).reshape(2, 128, 128)
    w0 = lax.all_gather(w_proj[0], "ch", axis=0)
    small = three(jnp.stack([out_gain, out_bias, pair_bias])).reshape(18, 32)
    packed = jnp.concatenate(
        [
            w_proj[1],
            w_gate.transpose(0, 2, 1).reshape(64, 128),
            w_out.reshape(64, 128),
            jnp.pad(small, ((0, 14), (0, 96))),
        ],
        axis=0,
    )
    gains = jnp.concatenate([in_gain.T, in_bias.T], axis=1)

    mask = by_plane(residue_mask.astype(f32)).reshape(8, 16)
    chain = by_plane(chain_ids).reshape(8, 16)
    mine = ix * 2 + iyh
    mask_r = lax.dynamic_index_in_dim(mask, mine, 0, keepdims=False)
    chain_r = lax.dynamic_index_in_dim(chain, mine, 0, keepdims=False)
    mask_c = lax.dynamic_index_in_dim(mask.reshape(4, 32), q, 0, keepdims=False)
    chain_c = lax.dynamic_index_in_dim(chain.reshape(4, 32), q, 0, keepdims=False)
    pm = (mask_r[:, None] * mask_c[None, :]).reshape(1, 512)
    same = (chain_r[:, None] == chain_c[None, :]).astype(f32).reshape(1, 512)

    send, z0, n0 = call(
        first_kernel,
        [((32, 32, 128), bf16), ((128, 512), f32), ((128, 512), bf16)],
        [got, gains, w0, pm],
        [(1024, 128)],
    )
    send, packed = lax.optimization_barrier((send, packed))
    got = lax.all_to_all(send, PLANE, 0, 0, tiled=True)
    packed = lax.all_gather(packed, "ch", axis=0)
    cols = packed[:, 256:274, :32].reshape(4, 3, 6, 32).astype(f32).sum(axis=1)
    cols = cols.transpose(0, 2, 1).reshape(128, 6)
    (gate,) = call(gate_kernel, [((128, 512), f32)], [n0, packed, cols, same])
    (send,) = call(outgoing_kernel, [((32, 16, 128), bf16)], [got])
    got = lax.all_to_all(send, PLANE, 0, 0, tiled=True)
    send, z1, n1 = call(
        middle_kernel,
        [((32, 32, 128), bf16), ((128, 512), bf16), ((128, 512), bf16)],
        [got, z0, gate, gains, cols, packed, pm],
        [(1024, 128), (512, 128)],
    )
    got = lax.all_to_all(send, PLANE, 0, 0, tiled=True)
    (zg,) = call(own_kernel, [((128, 128), bf16)], [z1, n1, packed, cols, same])
    (send,) = call(incoming_kernel, [((32, 8, 128), bf16)], [got], [(256, 128)])
    send, zg = lax.optimization_barrier((send, zg))
    got = lax.all_to_all(send, PLANE, 0, 0, tiled=True)
    zg = lax.all_gather(zg, "ch", axis=0)
    (out,) = call(
        last_kernel, [((32, 128), bf16)], [got, zg, packed, cols], [(256, 128), (128, 128)]
    )
    return out.reshape(32, 1, 128)


def solution(mesh):
    fine = Mesh(mesh.devices.reshape(4, 16, 2, 4), ("x", "z", "yh", "ch"))
    return jax.shard_map(
        body,
        mesh=fine,
        in_specs=(
            P("ch", ROW, None),
            P(),
            P(),
            P(),
            P(),
            P(None, None, None, "ch"),
            P(None, None, "ch"),
            P(None, "ch"),
            P(None, "ch"),
            P(None, "ch"),
            P(None, "ch", None),
        ),
        out_specs=P("ch", ROW, None),
        check_vma=False,
    )
```

```python
import jax
import jax.numpy as jnp
from jax import lax
from jax.experimental import pallas as pl
from jax.experimental.pallas import tpu as pltpu
from jax.sharding import Mesh, PartitionSpec as P

epsilon = 1e-05
bf16 = jnp.bfloat16
f32 = jnp.float32
ROW = ("x", "z", "yh")
PLANE = ("x", "yh", "ch")
VMEM = pl.BlockSpec(memory_space=pltpu.VMEM)
HBM = pl.BlockSpec(memory_space=pltpu.HBM)


def call(kernel, outs, ins, scratch=(), flops=100_000_000):
    moved = sum(a.size * a.dtype.itemsize for a in ins)
    return pl.pallas_call(
        kernel,
        out_shape=[jax.ShapeDtypeStruct(s, d) for s, d in outs],
        in_specs=[VMEM] * len(ins),
        out_specs=[VMEM] * len(outs),
        scratch_shapes=[pltpu.VMEM(s, f32) for s in scratch],
        compiler_params=pltpu.CompilerParams(vmem_limit_bytes=32 * 1024 * 1024),
        cost_estimate=pl.CostEstimate(flops=flops, bytes_accessed=moved, transcendentals=0),
    )(*ins)


def tn(a, b):
    return lax.dot_general(a, b, (((0,), (0,)), ((), ())), preferred_element_type=f32)


def nt(a, b):
    return lax.dot_general(a, b, (((1,), (1,)), ((), ())), preferred_element_type=f32)


def sigmoid(v):
    return 0.5 * jnp.tanh(0.5 * v) + 0.5


def norm(v, gain, bias):
    mean = jnp.mean(v, axis=0, keepdims=True)
    var = jnp.mean(v * v, axis=0, keepdims=True) - mean * mean
    return ((v - mean) * lax.rsqrt(var + epsilon) * gain + bias).astype(bf16)


def lanes(pieces):
    return jnp.concatenate(pieces, axis=1)


def permutation():
    k = lax.broadcasted_iota(jnp.int32, (128, 128), 0)
    p = lax.broadcasted_iota(jnp.int32, (128, 128), 1)
    place = (k & 96) | ((k & 1) << 4) | ((k & 31) >> 1)
    return (place == p).astype(f32).astype(bf16)


def spread_kernel(x_ref, out_ref, tile, sems):
    t = jnp.dot(x_ref[...], permutation(), preferred_element_type=f32)
    for q in range(4):
        piece = lanes([t[c * 8 : c * 8 + 8, q * 32 : q * 32 + 32] for c in range(4)])
        tile[q] = piece.astype(bf16)
    copies = [pltpu.make_async_copy(tile, out_ref.at[z * 4 : z * 4 + 4], sems.at[z]) for z in range(16)]
    for c in copies:
        c.start()
    for c in copies:
        c.wait()


def spread(x):
    return pl.pallas_call(
        spread_kernel,
        out_shape=jax.ShapeDtypeStruct((64, 8, 128), bf16),
        in_specs=[VMEM],
        out_specs=HBM,
        scratch_shapes=[pltpu.VMEM((4, 8, 128), bf16), pltpu.SemaphoreType.DMA((16,))],
    )(x)


def project(n, w_ref, u, pm, out_ref):
    sides = ([], [])
    for q in range(4):
        w = w_ref[q, u * 128 : u * 128 + 128, :]
        p = jnp.dot(w, n, preferred_element_type=f32)
        sides[0].append(sigmoid(p[0:32]) * p[32:64] * pm)
        sides[1].append(sigmoid(p[64:96]) * p[96:128] * pm)
    for s in range(2):
        v = jnp.stack([lanes([v[:, z * 32 : z * 32 + 32] for v in sides[s]]) for z in range(16)], axis=0)
        out_ref[:, s * 16 : s * 16 + 16, :] = jnp.swapaxes(v, 0, 1).astype(bf16)


def gates(n, w_ref, u, cols, same):
    w = jnp.concatenate([w_ref[q, 256 + u * 32 : 288 + u * 32, :] for q in range(4)], axis=0)
    return sigmoid(jnp.dot(w, n, preferred_element_type=f32) + cols * same)


def first_kernel(got_ref, gain_ref, cols_ref, w_ref, pm_ref, same_ref, out_ref, z_ref, gate_ref):
    rows = []
    for q in range(4):
        for c in range(4):
            pieces = [got_ref[z * 4 + q].astype(f32)[:, c * 32 : c * 32 + 32] for z in range(16)]
            rows.append(lanes(pieces))
    z0 = jnp.concatenate(rows, axis=0)
    z_ref[...] = z0
    n = norm(z0, gain_ref[:, 0:1], gain_ref[:, 2:3])
    gate_ref[...] = gates(n, w_ref, 0, cols_ref[:, 4:5], same_ref[...])
    project(n, w_ref, 0, pm_ref[...], out_ref)


def outgoing_kernel(got_ref, out_ref):
    row = lax.broadcasted_iota(jnp.int32, (128, 512), 0) >> 5
    lane = (lax.broadcasted_iota(jnp.int32, (128, 512), 1) >> 5) & 3
    same = row == lane
    left, right = [], []
    for q in range(4):
        left.append(jnp.concatenate([got_ref[a * 4 + q, 0:16, :] for a in range(8)], axis=0))
        right.append(jnp.concatenate([got_ref[a * 4 + q, 16:32, :] for a in range(8)], axis=0))
    left, right = lanes(left), lanes(right)
    for q in range(4):
        part = right[q * 32 : q * 32 + 32].astype(f32)
        block = jnp.where(same, jnp.concatenate([part] * 4, axis=0), 0.0).astype(bf16)
        x = nt(left, block).astype(bf16)
        for b in range(8):
            out_ref[b * 4 + q] = x[b * 16 : b * 16 + 16]


def middle_kernel(got_ref, z_ref, gate_ref, gain_ref, cols_ref, w_ref, pm_ref, out_ref, z1_ref, n1_ref):
    x = jnp.swapaxes(got_ref[...].astype(f32), 0, 1)
    x0 = jnp.concatenate(
        [lanes([x[z][:, d * 32 : d * 32 + 32] for z in range(16)]) for d in range(4)], axis=0
    )
    xn = norm(x0, cols_ref[:, 0:1], cols_ref[:, 2:3])
    w = jnp.concatenate([w_ref[q, 320:352, :] for q in range(4)], axis=0)
    z1 = (z_ref[...] + gate_ref[...] * tn(w, xn)).astype(bf16)
    z1_ref[...] = z1
    n1 = norm(z1.astype(f32), gain_ref[:, 1:2], gain_ref[:, 3:4])
    n1_ref[...] = n1
    project(n1, w_ref, 1, pm_ref[...], out_ref)


def incoming_kernel(got_ref, z1_ref, n1_ref, cols_ref, w_ref, same_ref, out_ref):
    here = lax.axis_index("z")
    left, right = [], []
    for q in range(4):
        left.append(jnp.concatenate([got_ref[a * 4 + q, 0:16, :] for a in range(8)], axis=0))
        right.append(jnp.concatenate([got_ref[a * 4 + q, 16:32, :] for a in range(8)], axis=0))
    row = lax.broadcasted_iota(jnp.int32, (32, 512), 0)
    lane = lax.broadcasted_iota(jnp.int32, (32, 512), 1)
    want = (((row >> 1) & 3) << 7) | ((row >> 3) << 5) | ((row & 1) << 4) | here
    pick = (lane == want).astype(f32).astype(bf16)
    mine = nt(pick, lanes(left)).astype(bf16)
    prods = [jnp.dot(mine, r, preferred_element_type=f32) for r in right]
    xs = [lanes([p[d * 8 : d * 8 + 8, d * 32 : d * 32 + 32] for p in prods]) for d in range(4)]
    x = jnp.swapaxes(jnp.stack(xs + xs, axis=0), 0, 1).astype(bf16)
    lane = lax.broadcasted_iota(jnp.int32, (512, 128), 0)
    col = lax.broadcasted_iota(jnp.int32, (512, 128), 1)
    pick = ((lane == here * 32 + col) & (col < 32)).astype(f32).astype(bf16)
    z1 = jnp.dot(z1_ref[...], pick, preferred_element_type=f32)
    n1 = jnp.dot(n1_ref[...], pick, preferred_element_type=f32).astype(bf16)
    same = jnp.dot(
        jnp.broadcast_to(same_ref[...], (8, 512)).astype(bf16), pick, preferred_element_type=f32
    )[0:1]
    gate = gates(n1, w_ref, 1, cols_ref[:, 5:6], same)
    for q in range(4):
        zq, gq = (
            lanes([v[q * 32 + c * 8 : q * 32 + c * 8 + 8, 0:32] for c in range(4)]).astype(bf16)
            for v in (z1, gate)
        )
        for a in range(8):
            out_ref[a * 4 + q, 0:8, :] = x[a]
            out_ref[a * 4 + q, 8:16, :] = zq
            out_ref[a * 4 + q, 16:24, :] = gq


def last_kernel(got_ref, cols_ref, w_ref, out_ref, ys):
    x = jnp.swapaxes(got_ref[:, 0:8, :].astype(f32), 0, 1)
    x1 = jnp.concatenate([x[d] for d in range(4)], axis=0)
    xn = norm(x1, cols_ref[:, 1:2], cols_ref[:, 3:4])
    w = jnp.concatenate([w_ref[q, 352:384, :] for q in range(4)], axis=0)
    ys[...] = tn(w, xn)
    y = ys[pl.ds(pl.multiple_of(lax.axis_index("ch") * 32, 32), 32), :]
    home = (lax.axis_index("x") * 2 + lax.axis_index("yh")) * 4
    own = [got_ref[home + s].astype(f32) for s in range(4)]
    z1, gate = (
        jnp.concatenate(
            [lanes([o[r : r + 8, c * 32 : c * 32 + 32] for o in own]) for c in range(4)], axis=0
        )
        for r in (8, 16)
    )
    out = (z1 + gate * y).astype(bf16)
    out_ref[...] = nt(out, permutation()).astype(bf16)


def three(v):
    hi = lax.reduce_precision(v, 8, 7)
    mid = lax.reduce_precision(v - hi, 8, 7)
    return jnp.stack([hi, mid, v - hi - mid]).astype(bf16)


def by_plane(v):
    return v.reshape(4, 16, 2).swapaxes(1, 2).reshape(128)


def body(pair_rep, residue_mask, chain_ids, in_gain, in_bias, w_proj, w_gate, pair_bias, out_gain, out_bias, w_out):
    ix, iyh, q = (lax.axis_index(a) for a in ("x", "yh", "ch"))
    send = spread(pair_rep.reshape(32, 128))
    got = lax.all_to_all(send, ("z", "ch"), 0, 0, tiled=True)

    w_proj = w_proj.transpose(0, 2, 3, 1).reshape(2, 128, 128)
    small = three(jnp.stack([out_gain, out_bias, pair_bias])).reshape(18, 32)
    packed = jnp.concatenate(
        [
            w_proj.reshape(256, 128),
            w_gate.transpose(0, 2, 1).reshape(64, 128),
            w_out.reshape(64, 128),
            jnp.pad(small, ((0, 14), (0, 96))),
        ],
        axis=0,
    )
    packed = lax.all_gather(packed, "ch", axis=0)
    cols = packed[:, 384:402, :32].reshape(4, 3, 6, 32).astype(f32).sum(axis=1)
    cols = cols.transpose(0, 2, 1).reshape(128, 6)
    gains = jnp.concatenate([in_gain.T, in_bias.T], axis=1)

    mask = by_plane(residue_mask.astype(f32)).reshape(8, 16)
    chain = by_plane(chain_ids).reshape(8, 16)
    mine = ix * 2 + iyh
    mask_r = lax.dynamic_index_in_dim(mask, mine, 0, keepdims=False)
    chain_r = lax.dynamic_index_in_dim(chain, mine, 0, keepdims=False)
    mask_c = lax.dynamic_index_in_dim(mask.reshape(4, 32), q, 0, keepdims=False)
    chain_c = lax.dynamic_index_in_dim(chain.reshape(4, 32), q, 0, keepdims=False)
    pm = (mask_r[:, None] * mask_c[None, :]).reshape(1, 512)
    same = (chain_r[:, None] == chain_c[None, :]).astype(f32).reshape(1, 512)

    got, packed, cols, gains, pm, same = lax.optimization_barrier((got, packed, cols, gains, pm, same))
    send, z0, gate = call(
        first_kernel,
        [((32, 32, 128), bf16), ((128, 512), f32), ((128, 512), f32)],
        [got, gains, cols, packed, pm, same],
    )
    got = lax.all_to_all(send, PLANE, 0, 0, tiled=True)
    (send,) = call(outgoing_kernel, [((32, 16, 128), bf16)], [got])
    got = lax.all_to_all(send, PLANE, 0, 0, tiled=True)
    send, z1, n1 = call(
        middle_kernel,
        [((32, 32, 128), bf16), ((128, 512), bf16), ((128, 512), bf16)],
        [got, z0, gate, gains, cols, packed, pm],
    )
    got = lax.all_to_all(send, PLANE, 0, 0, tiled=True)
    (send,) = call(incoming_kernel, [((32, 24, 128), bf16)], [got, z1, n1, cols, packed, same])
    got = lax.all_to_all(send, PLANE, 0, 0, tiled=True)
    (out,) = call(last_kernel, [((32, 128), bf16)], [got, cols, packed], [(128, 128)])
    return out.reshape(32, 1, 128)


def solution(mesh):
    fine = Mesh(mesh.devices.reshape(4, 16, 2, 4), ("x", "z", "yh", "ch"))
    return jax.shard_map(
        body,
        mesh=fine,
        in_specs=(
            P("ch", ROW, None),
            P(),
            P(),
            P(),
            P(),
            P(None, None, None, "ch"),
            P(None, None, "ch"),
            P(None, "ch"),
            P(None, "ch"),
            P(None, "ch"),
            P(None, "ch", None),
        ),
        out_specs=P("ch", ROW, None),
        check_vma=False,
    )
```

```python
import jax
import jax.numpy as jnp
from jax import lax
from jax.experimental import pallas as pl
from jax.experimental.pallas import tpu as pltpu
from jax.sharding import Mesh, PartitionSpec as P

epsilon = 1e-05
bf16 = jnp.bfloat16
f32 = jnp.float32
ROW = ("x", "z", "yh")
PLANE = ("x", "yh", "ch")
VMEM = pl.BlockSpec(memory_space=pltpu.VMEM)
HBM = pl.BlockSpec(memory_space=pltpu.HBM)


def call(kernel, outs, ins, scratch=(), flops=100_000_000):
    moved = sum(a.size * a.dtype.itemsize for a in ins)
    return pl.pallas_call(
        kernel,
        out_shape=[jax.ShapeDtypeStruct(s, d) for s, d in outs],
        in_specs=[VMEM] * len(ins),
        out_specs=[VMEM] * len(outs),
        scratch_shapes=[pltpu.VMEM(s, f32) for s in scratch],
        compiler_params=pltpu.CompilerParams(vmem_limit_bytes=32 * 1024 * 1024),
        cost_estimate=pl.CostEstimate(flops=flops, bytes_accessed=moved, transcendentals=0),
    )(*ins)


def tn(a, b):
    return lax.dot_general(a, b, (((0,), (0,)), ((), ())), preferred_element_type=f32)


def nt(a, b):
    return lax.dot_general(a, b, (((1,), (1,)), ((), ())), preferred_element_type=f32)


def sigmoid(v):
    return 0.5 * jnp.tanh(0.5 * v) + 0.5


def norm(v, gain, bias):
    mean = jnp.mean(v, axis=0, keepdims=True)
    var = jnp.mean(v * v, axis=0, keepdims=True) - mean * mean
    return ((v - mean) * lax.rsqrt(var + epsilon) * gain + bias).astype(bf16)


def lanes(pieces):
    return jnp.concatenate(pieces, axis=1)


def permutation():
    k = lax.broadcasted_iota(jnp.int32, (128, 128), 0)
    p = lax.broadcasted_iota(jnp.int32, (128, 128), 1)
    place = (k & 96) | ((k & 1) << 4) | ((k & 31) >> 1)
    return (place == p).astype(f32).astype(bf16)


def spread_kernel(x_ref, out_ref, tile, sems):
    t = jnp.dot(x_ref[...], permutation(), preferred_element_type=f32)
    for q in range(4):
        piece = lanes([t[c * 8 : c * 8 + 8, q * 32 : q * 32 + 32] for c in range(4)])
        tile[q] = piece.astype(bf16)
    copies = [pltpu.make_async_copy(tile, out_ref.at[z * 4 : z * 4 + 4], sems.at[z]) for z in range(16)]
    for c in copies:
        c.start()
    for c in copies:
        c.wait()


def spread(x):
    return pl.pallas_call(
        spread_kernel,
        out_shape=jax.ShapeDtypeStruct((64, 8, 128), bf16),
        in_specs=[VMEM],
        out_specs=HBM,
        scratch_shapes=[pltpu.VMEM((4, 8, 128), bf16), pltpu.SemaphoreType.DMA((16,))],
        compiler_params=pltpu.CompilerParams(vmem_limit_bytes=32 * 1024 * 1024),
    )(x)


def prepare_kernel(
    mask_ref, chain_ref, gain_ref, bias_ref, pb_ref, og_ref, ob_ref, wp_ref, wg_ref, wo_ref,
    packed_ref, gains_ref, pm_ref, same_ref, marks, inner, outer, sems,
):
    places = [
        (wp_ref, packed_ref.at[0:256]),
        (wg_ref, packed_ref.at[256:320]),
        (wo_ref, packed_ref.at[320:384]),
        (mask_ref, marks.at[0:1]),
        (chain_ref, marks.at[1:2]),
        (gain_ref, inner.at[0:2]),
        (bias_ref, inner.at[2:4]),
        (og_ref, outer.at[0]),
        (ob_ref, outer.at[1]),
        (pb_ref, outer.at[2]),
    ]
    copies = [pltpu.make_async_copy(a, b, sems.at[i]) for i, (a, b) in enumerate(places)]
    for c in copies[3:] + copies[:3]:
        c.start()
    ix, iyh, q = (lax.axis_index(a) for a in ("x", "yh", "ch"))
    place = lax.broadcasted_iota(jnp.int32, (128, 512), 0)
    pair = lax.broadcasted_iota(jnp.int32, (128, 512), 1)
    rows = place == (ix * 32 + iyh) + ((pair >> 5) << 1)
    columns = place == q * 32 + (((pair & 15) << 1) | ((pair >> 4) & 1))
    rows, columns = (v.astype(f32).astype(bf16) for v in (rows, columns))
    for c in copies[3:]:
        c.wait()
    m = marks[0:2, :].astype(f32)
    m = jnp.concatenate([m, jnp.zeros((6, 128), f32)], axis=0).astype(bf16)
    r = jnp.dot(m, rows, preferred_element_type=f32)
    c = jnp.dot(m, columns, preferred_element_type=f32)
    pm_ref[...] = r[0:1] * c[0:1]
    same_ref[...] = (r[1:2] == c[1:2]).astype(f32)
    g = jnp.concatenate([inner[0:4, :], jnp.zeros((124, 128), f32)], axis=0)
    gains_ref[...] = g.T[:, 0:8]
    v = jnp.concatenate([outer[i] for i in range(3)], axis=0)
    hi = v.astype(bf16).astype(f32)
    mid = (v - hi).astype(bf16).astype(f32)
    low = v - hi - mid
    v = jnp.concatenate([hi, mid, low, jnp.zeros((110, 32), f32)], axis=0)
    v = lanes([v, jnp.zeros((128, 96), f32)])
    packed_ref[384:416, :] = v.T[0:32].astype(bf16)
    for c in copies[:3]:
        c.wait()


def prepare(*args):
    return pl.pallas_call(
        prepare_kernel,
        out_shape=[
            jax.ShapeDtypeStruct((416, 128), bf16),
            jax.ShapeDtypeStruct((128, 8), f32),
            jax.ShapeDtypeStruct((1, 512), f32),
            jax.ShapeDtypeStruct((1, 512), f32),
        ],
        in_specs=[HBM] * 10,
        out_specs=[VMEM] * 4,
        scratch_shapes=[
            pltpu.VMEM((2, 128), jnp.int32),
            pltpu.VMEM((4, 128), f32),
            pltpu.VMEM((3, 2, 32), f32),
            pltpu.SemaphoreType.DMA((10,)),
        ],
        compiler_params=pltpu.CompilerParams(vmem_limit_bytes=32 * 1024 * 1024),
    )(*args)


def columns_of(w_ref):
    v = jnp.concatenate([w_ref[q, 384:416, :].astype(f32) for q in range(4)], axis=0)
    return v[:, 0:6] + v[:, 6:12] + v[:, 12:18]


def project(n, w_ref, u, pm, out_ref):
    sides = ([], [])
    for q in range(4):
        w = w_ref[q, u * 128 : u * 128 + 128, :]
        p = jnp.dot(w, n, preferred_element_type=f32)
        sides[0].append(sigmoid(p[0:32]) * p[32:64] * pm)
        sides[1].append(sigmoid(p[64:96]) * p[96:128] * pm)
    for s in range(2):
        v = jnp.stack([lanes([v[:, z * 32 : z * 32 + 32] for v in sides[s]]) for z in range(16)], axis=0)
        out_ref[:, s * 16 : s * 16 + 16, :] = jnp.swapaxes(v, 0, 1).astype(bf16)


def gates(n, w_ref, u, cols, same):
    w = jnp.concatenate([w_ref[q, 256 + u * 32 : 288 + u * 32, :] for q in range(4)], axis=0)
    return sigmoid(jnp.dot(w, n, preferred_element_type=f32) + cols * same)


def first_kernel(got_ref, gain_ref, w_ref, pm_ref, same_ref, out_ref, z_ref, gate_ref):
    rows = []
    for q in range(4):
        for c in range(4):
            pieces = [got_ref[z * 4 + q].astype(f32)[:, c * 32 : c * 32 + 32] for z in range(16)]
            rows.append(lanes(pieces))
    z0 = jnp.concatenate(rows, axis=0)
    z_ref[...] = z0
    n = norm(z0, gain_ref[:, 0:1], gain_ref[:, 2:3])
    gate_ref[...] = gates(n, w_ref, 0, columns_of(w_ref)[:, 4:5], same_ref[...])
    project(n, w_ref, 0, pm_ref[...], out_ref)


def outgoing_kernel(got_ref, out_ref):
    row = lax.broadcasted_iota(jnp.int32, (128, 512), 0) >> 5
    lane = (lax.broadcasted_iota(jnp.int32, (128, 512), 1) >> 5) & 3
    same = row == lane
    left, right = [], []
    for q in range(4):
        left.append(jnp.concatenate([got_ref[a * 4 + q, 0:16, :] for a in range(8)], axis=0))
        right.append(jnp.concatenate([got_ref[a * 4 + q, 16:32, :] for a in range(8)], axis=0))
    left, right = lanes(left), lanes(right)
    for q in range(4):
        part = right[q * 32 : q * 32 + 32].astype(f32)
        block = jnp.where(same, jnp.concatenate([part] * 4, axis=0), 0.0).astype(bf16)
        x = nt(left, block).astype(bf16)
        for b in range(8):
            out_ref[b * 4 + q] = x[b * 16 : b * 16 + 16]


def middle_kernel(got_ref, z_ref, gate_ref, gain_ref, w_ref, pm_ref, out_ref, z1_ref, n1_ref):
    x = jnp.swapaxes(got_ref[...].astype(f32), 0, 1)
    x0 = jnp.concatenate(
        [lanes([x[z][:, d * 32 : d * 32 + 32] for z in range(16)]) for d in range(4)], axis=0
    )
    cols = columns_of(w_ref)
    xn = norm(x0, cols[:, 0:1], cols[:, 2:3])
    w = jnp.concatenate([w_ref[q, 320:352, :] for q in range(4)], axis=0)
    z1 = (z_ref[...] + gate_ref[...] * tn(w, xn)).astype(bf16)
    z1_ref[...] = z1
    n1 = norm(z1.astype(f32), gain_ref[:, 1:2], gain_ref[:, 3:4])
    n1_ref[...] = n1
    project(n1, w_ref, 1, pm_ref[...], out_ref)


def incoming_kernel(got_ref, z1_ref, n1_ref, w_ref, same_ref, out_ref):
    here = lax.axis_index("z")
    left, right = [], []
    for q in range(4):
        left.append(jnp.concatenate([got_ref[a * 4 + q, 0:16, :] for a in range(8)], axis=0))
        right.append(jnp.concatenate([got_ref[a * 4 + q, 16:32, :] for a in range(8)], axis=0))
    row = lax.broadcasted_iota(jnp.int32, (32, 512), 0)
    lane = lax.broadcasted_iota(jnp.int32, (32, 512), 1)
    want = (((row >> 1) & 3) << 7) | ((row >> 3) << 5) | ((row & 1) << 4) | here
    pick = (lane == want).astype(f32).astype(bf16)
    mine = nt(pick, lanes(left)).astype(bf16)
    prods = [jnp.dot(mine, r, preferred_element_type=f32) for r in right]
    xs = [lanes([p[d * 8 : d * 8 + 8, d * 32 : d * 32 + 32] for p in prods]) for d in range(4)]
    x = jnp.swapaxes(jnp.stack(xs + xs, axis=0), 0, 1).astype(bf16)
    lane = lax.broadcasted_iota(jnp.int32, (512, 128), 0)
    col = lax.broadcasted_iota(jnp.int32, (512, 128), 1)
    pick = ((lane == here * 32 + col) & (col < 32)).astype(f32).astype(bf16)
    z1 = jnp.dot(z1_ref[...], pick, preferred_element_type=f32)
    n1 = jnp.dot(n1_ref[...], pick, preferred_element_type=f32).astype(bf16)
    same = jnp.dot(
        jnp.broadcast_to(same_ref[...], (8, 512)).astype(bf16), pick, preferred_element_type=f32
    )[0:1]
    gate = gates(n1, w_ref, 1, columns_of(w_ref)[:, 5:6], same)
    for q in range(4):
        zq, gq = (
            lanes([v[q * 32 + c * 8 : q * 32 + c * 8 + 8, 0:32] for c in range(4)]).astype(bf16)
            for v in (z1, gate)
        )
        for a in range(8):
            out_ref[a * 4 + q, 0:8, :] = x[a]
            out_ref[a * 4 + q, 8:16, :] = zq
            out_ref[a * 4 + q, 16:24, :] = gq


def last_kernel(got_ref, w_ref, out_ref, ys):
    x = jnp.swapaxes(got_ref[:, 0:8, :].astype(f32), 0, 1)
    x1 = jnp.concatenate([x[d] for d in range(4)], axis=0)
    cols = columns_of(w_ref)
    xn = norm(x1, cols[:, 1:2], cols[:, 3:4])
    w = jnp.concatenate([w_ref[q, 352:384, :] for q in range(4)], axis=0)
    ys[...] = tn(w, xn)
    y = ys[pl.ds(pl.multiple_of(lax.axis_index("ch") * 32, 32), 32), :]
    home = (lax.axis_index("x") * 2 + lax.axis_index("yh")) * 4
    own = [got_ref[home + s].astype(f32) for s in range(4)]
    z1, gate = (
        jnp.concatenate(
            [lanes([o[r : r + 8, c * 32 : c * 32 + 32] for o in own]) for c in range(4)], axis=0
        )
        for r in (8, 16)
    )
    out = (z1 + gate * y).astype(bf16)
    out_ref[...] = nt(out, permutation()).astype(bf16)


def body(pair_rep, residue_mask, chain_ids, in_gain, in_bias, w_proj, w_gate, pair_bias, out_gain, out_bias, w_out):
    send = spread(pair_rep.reshape(32, 128))
    args = (
        residue_mask.reshape(1, 128),
        chain_ids.reshape(1, 128),
        in_gain,
        in_bias,
        pair_bias,
        out_gain,
        out_bias,
        w_proj.transpose(0, 2, 3, 1).reshape(256, 128),
        w_gate.transpose(0, 2, 1).reshape(64, 128),
        w_out.reshape(64, 128),
    )
    send, *args = lax.optimization_barrier((send, *args))
    got = lax.all_to_all(send, ("z", "ch"), 0, 0, tiled=True)
    packed, gains, pm, same = prepare(*args)
    packed = lax.all_gather(packed, "ch", axis=0)
    got, packed, gains, pm, same = lax.optimization_barrier((got, packed, gains, pm, same))
    send, z0, gate = call(
        first_kernel,
        [((32, 32, 128), bf16), ((128, 512), f32), ((128, 512), f32)],
        [got, gains, packed, pm, same],
    )
    got = lax.all_to_all(send, PLANE, 0, 0, tiled=True)
    (send,) = call(outgoing_kernel, [((32, 16, 128), bf16)], [got])
    got = lax.all_to_all(send, PLANE, 0, 0, tiled=True)
    send, z1, n1 = call(
        middle_kernel,
        [((32, 32, 128), bf16), ((128, 512), bf16), ((128, 512), bf16)],
        [got, z0, gate, gains, packed, pm],
    )
    got = lax.all_to_all(send, PLANE, 0, 0, tiled=True)
    (send,) = call(incoming_kernel, [((32, 24, 128), bf16)], [got, z1, n1, packed, same])
    got = lax.all_to_all(send, PLANE, 0, 0, tiled=True)
    (out,) = call(last_kernel, [((32, 128), bf16)], [got, packed], [(128, 128)])
    return out.reshape(32, 1, 128)


def solution(mesh):
    fine = Mesh(mesh.devices.reshape(4, 16, 2, 4), ("x", "z", "yh", "ch"))
    return jax.shard_map(
        body,
        mesh=fine,
        in_specs=(
            P("ch", ROW, None),
            P(),
            P(),
            P(),
            P(),
            P(None, None, None, "ch"),
            P(None, None, "ch"),
            P(None, "ch"),
            P(None, "ch"),
            P(None, "ch"),
            P(None, "ch", None),
        ),
        out_specs=P("ch", ROW, None),
        check_vma=False,
    )
```

```python
import jax
import jax.numpy as jnp
from jax import lax
from jax.experimental import pallas as pl
from jax.experimental.pallas import tpu as pltpu
from jax.sharding import Mesh, PartitionSpec as P

epsilon = 1e-05
bf16 = jnp.bfloat16
f32 = jnp.float32
ROW = ("x", "z", "yh")
PLANE = ("x", "yh", "ch")
VMEM = pl.BlockSpec(memory_space=pltpu.VMEM)
HBM = pl.BlockSpec(memory_space=pltpu.HBM)


def call(kernel, outs, ins, scratch=(), flops=100_000_000):
    moved = sum(a.size * a.dtype.itemsize for a in ins)
    return pl.pallas_call(
        kernel,
        out_shape=[jax.ShapeDtypeStruct(s, d) for s, d in outs],
        in_specs=[VMEM] * len(ins),
        out_specs=[VMEM] * len(outs),
        scratch_shapes=[pltpu.VMEM(s, f32) for s in scratch],
        compiler_params=pltpu.CompilerParams(vmem_limit_bytes=32 * 1024 * 1024),
        cost_estimate=pl.CostEstimate(flops=flops, bytes_accessed=moved, transcendentals=0),
    )(*ins)


def tn(a, b):
    return lax.dot_general(a, b, (((0,), (0,)), ((), ())), preferred_element_type=f32)


def nt(a, b):
    return lax.dot_general(a, b, (((1,), (1,)), ((), ())), preferred_element_type=f32)


def sigmoid(v):
    return 0.5 * jnp.tanh(0.5 * v) + 0.5


def norm(v, gain, bias):
    mean = jnp.mean(v, axis=0, keepdims=True)
    var = jnp.mean(v * v, axis=0, keepdims=True) - mean * mean
    return ((v - mean) * lax.rsqrt(var + epsilon) * gain + bias).astype(bf16)


def lanes(pieces):
    return jnp.concatenate(pieces, axis=1)


def permutation():
    k = lax.broadcasted_iota(jnp.int32, (128, 128), 0)
    p = lax.broadcasted_iota(jnp.int32, (128, 128), 1)
    place = (k & 96) | ((k & 1) << 4) | ((k & 31) >> 1)
    return (place == p).astype(f32).astype(bf16)


def spread_kernel(x_ref, out_ref, tile, sems):
    t = jnp.dot(x_ref[...], permutation(), preferred_element_type=f32)
    for q in range(4):
        piece = lanes([t[c * 8 : c * 8 + 8, q * 32 : q * 32 + 32] for c in range(4)])
        tile[q] = piece.astype(bf16)
    copies = [pltpu.make_async_copy(tile, out_ref.at[z * 4 : z * 4 + 4], sems.at[z]) for z in range(16)]
    for c in copies:
        c.start()
    for c in copies:
        c.wait()


def spread(x):
    return pl.pallas_call(
        spread_kernel,
        out_shape=jax.ShapeDtypeStruct((64, 8, 128), bf16),
        in_specs=[VMEM],
        out_specs=HBM,
        scratch_shapes=[pltpu.VMEM((4, 8, 128), bf16), pltpu.SemaphoreType.DMA((16,))],
        compiler_params=pltpu.CompilerParams(vmem_limit_bytes=32 * 1024 * 1024),
    )(x)


def prepare_kernel(
    mask_ref, chain_ref, gain_ref, bias_ref, pb_ref, og_ref, ob_ref, wp_ref, wg_ref, wo_ref,
    packed_ref, gains_ref, pm_ref, same_ref, marks, inner, outer, sems,
):
    places = [
        (wp_ref, packed_ref.at[0:256]),
        (wg_ref, packed_ref.at[256:320]),
        (wo_ref, packed_ref.at[320:384]),
        (mask_ref, marks.at[0:1]),
        (chain_ref, marks.at[1:2]),
        (gain_ref, inner.at[0:2]),
        (bias_ref, inner.at[2:4]),
        (og_ref, outer.at[0]),
        (ob_ref, outer.at[1]),
        (pb_ref, outer.at[2]),
    ]
    copies = [pltpu.make_async_copy(a, b, sems.at[i]) for i, (a, b) in enumerate(places)]
    for c in copies[3:] + copies[:3]:
        c.start()
    ix, iyh, q = (lax.axis_index(a) for a in ("x", "yh", "ch"))
    place = lax.broadcasted_iota(jnp.int32, (128, 512), 0)
    pair = lax.broadcasted_iota(jnp.int32, (128, 512), 1)
    rows = place == (ix * 32 + iyh) + ((pair >> 5) << 1)
    columns = place == q * 32 + (((pair & 15) << 1) | ((pair >> 4) & 1))
    rows, columns = (v.astype(f32).astype(bf16) for v in (rows, columns))
    for c in copies[3:]:
        c.wait()
    m = marks[0:2, :].astype(f32)
    m = jnp.concatenate([m, jnp.zeros((6, 128), f32)], axis=0).astype(bf16)
    r = jnp.dot(m, rows, preferred_element_type=f32)
    c = jnp.dot(m, columns, preferred_element_type=f32)
    pm_ref[...] = r[0:1] * c[0:1]
    same_ref[...] = (r[1:2] == c[1:2]).astype(f32)
    g = jnp.concatenate([inner[0:4, :], jnp.zeros((124, 128), f32)], axis=0)
    gains_ref[...] = g.T[:, 0:8]
    v = jnp.concatenate([outer[i] for i in range(3)], axis=0)
    hi = v.astype(bf16).astype(f32)
    mid = (v - hi).astype(bf16).astype(f32)
    low = v - hi - mid
    v = jnp.concatenate([hi, mid, low, jnp.zeros((110, 32), f32)], axis=0)
    v = lanes([v, jnp.zeros((128, 96), f32)])
    packed_ref[384:416, :] = v.T[0:32].astype(bf16)
    for c in copies[:3]:
        c.wait()


def prepare(*args):
    return pl.pallas_call(
        prepare_kernel,
        out_shape=[
            jax.ShapeDtypeStruct((416, 128), bf16),
            jax.ShapeDtypeStruct((128, 8), f32),
            jax.ShapeDtypeStruct((1, 512), f32),
            jax.ShapeDtypeStruct((1, 512), f32),
        ],
        in_specs=[HBM] * 10,
        out_specs=[VMEM] * 4,
        scratch_shapes=[
            pltpu.VMEM((2, 128), jnp.int32),
            pltpu.VMEM((4, 128), f32),
            pltpu.VMEM((3, 2, 32), f32),
            pltpu.SemaphoreType.DMA((10,)),
        ],
        compiler_params=pltpu.CompilerParams(vmem_limit_bytes=32 * 1024 * 1024),
    )(*args)


def columns_of(w_ref):
    v = jnp.concatenate([w_ref[q, 384:416, :].astype(f32) for q in range(4)], axis=0)
    return v[:, 0:6] + v[:, 6:12] + v[:, 12:18]


def project(n, w_ref, u, pm):
    sides = ([], [])
    for q in range(4):
        w = w_ref[q, u * 128 : u * 128 + 128, :]
        p = jnp.dot(w, n, preferred_element_type=f32)
        sides[0].append(sigmoid(p[0:32]) * p[32:64] * pm)
        sides[1].append(sigmoid(p[64:96]) * p[96:128] * pm)
    return sides


def slabs(v):
    return [lanes([a[:, z * 32 : z * 32 + 32] for a in v]) for z in range(16)]


def gates(n, w_ref, u, cols, same):
    w = jnp.concatenate([w_ref[q, 256 + u * 32 : 288 + u * 32, :] for q in range(4)], axis=0)
    return sigmoid(jnp.dot(w, n, preferred_element_type=f32) + cols * same)


def first_kernel(got_ref, gain_ref, w_ref, pm_ref, same_ref, out_ref, z_ref, gate_ref):
    rows = []
    for q in range(4):
        for c in range(4):
            pieces = [got_ref[z * 4 + q].astype(f32)[:, c * 32 : c * 32 + 32] for z in range(16)]
            rows.append(lanes(pieces))
    z0 = jnp.concatenate(rows, axis=0)
    z_ref[...] = z0
    n = norm(z0, gain_ref[:, 0:1], gain_ref[:, 2:3])
    gate_ref[...] = gates(n, w_ref, 0, columns_of(w_ref)[:, 4:5], same_ref[...])
    for s, v in enumerate(project(n, w_ref, 0, pm_ref[...])):
        v = jnp.swapaxes(jnp.stack(slabs(v), axis=0), 0, 1)
        out_ref[:, s * 16 : s * 16 + 16, :] = v.astype(bf16)


def outgoing_kernel(got_ref, out_ref):
    row = lax.broadcasted_iota(jnp.int32, (128, 512), 0) >> 5
    lane = (lax.broadcasted_iota(jnp.int32, (128, 512), 1) >> 5) & 3
    same = row == lane
    left, right = [], []
    for q in range(4):
        left.append(jnp.concatenate([got_ref[a * 4 + q, 0:16, :] for a in range(8)], axis=0))
        right.append(jnp.concatenate([got_ref[a * 4 + q, 16:32, :] for a in range(8)], axis=0))
    left, right = lanes(left), lanes(right)
    for q in range(4):
        part = right[q * 32 : q * 32 + 32].astype(f32)
        block = jnp.where(same, jnp.concatenate([part] * 4, axis=0), 0.0).astype(bf16)
        x = nt(left, block).astype(bf16)
        for b in range(8):
            out_ref[b * 4 + q] = x[b * 16 : b * 16 + 16]


def middle_kernel(got_ref, z_ref, gate_ref, gain_ref, w_ref, pm_ref, out_ref, z1_ref, n1_ref):
    x = jnp.swapaxes(got_ref[...].astype(f32), 0, 1)
    x0 = jnp.concatenate(
        [lanes([x[z][:, d * 32 : d * 32 + 32] for z in range(16)]) for d in range(4)], axis=0
    )
    cols = columns_of(w_ref)
    xn = norm(x0, cols[:, 0:1], cols[:, 2:3])
    w = jnp.concatenate([w_ref[q, 320:352, :] for q in range(4)], axis=0)
    z1 = (z_ref[...] + gate_ref[...] * tn(w, xn)).astype(bf16)
    z1_ref[...] = z1
    n1 = norm(z1.astype(f32), gain_ref[:, 1:2], gain_ref[:, 3:4])
    n1_ref[...] = n1
    left, right = project(n1, w_ref, 1, pm_ref[...])
    lane = lax.broadcasted_iota(jnp.int32, (512, 128), 0)
    col = lax.broadcasted_iota(jnp.int32, (512, 128), 1)
    want = ((col & 15) << 5) | (((col >> 4) & 1) << 4) | lax.axis_index("z")
    pick = ((lane == want) & (col < 32)).astype(f32).astype(bf16)
    left = lanes([jnp.dot(v.astype(bf16), pick, preferred_element_type=f32)[:, 0:32] for v in left])
    v = jnp.swapaxes(jnp.stack(slabs(right) + [left] * 8, axis=0), 0, 1)
    first = lax.broadcasted_iota(jnp.int32, (8, 128), 0) == 0
    for g in range(16):
        marks = jnp.where(first, v[g, 16:24], v[16 + g, 16:24]).astype(bf16)
        for yh in range(2):
            at = (g // 4) * 8 + yh * 4 + g % 4
            out_ref[at, 0:16, :] = v[g, 0:16].astype(bf16)
            out_ref[at, 16:32, :] = v[16 + g, 0:16].astype(bf16)
            out_ref[at, 32:40, :] = marks


def incoming_kernel(got_ref, z1_ref, n1_ref, w_ref, same_ref, out_ref):
    here = lax.axis_index("z")
    right = [
        lanes(
            [
                jnp.concatenate([got_ref[a * 4 + q, h * 16 : h * 16 + 16, :] for a in range(8)], axis=0)
                for h in range(2)
            ]
        )
        for q in range(4)
    ]
    row = lax.broadcasted_iota(jnp.int32, (32, 128), 0)
    lane = lax.broadcasted_iota(jnp.int32, (32, 128), 1)
    wanted = ((row >> 3) == (lane >> 5)) & (((lane >> 4) & 1) == lax.axis_index("yh"))
    parts = []
    for a in range(8):
        tiles = [got_ref[a * 4 + x, 32:40, :].astype(f32) for x in range(4)]
        rows = jnp.concatenate([t[h : h + 1] for h in range(2) for t in tiles], axis=0)
        parts.append(jnp.where(wanted, jnp.concatenate([rows] * 4, axis=0), 0.0).astype(bf16))
    source = lax.broadcasted_iota(jnp.int32, (1024, 128), 0)
    target = lax.broadcasted_iota(jnp.int32, (1024, 128), 1)
    place = ((source >> 7) << 4) | (source & 15)
    place = (place == target).astype(f32).astype(bf16)
    mine = jnp.dot(lanes(parts), place, preferred_element_type=f32).astype(bf16)
    prods = [jnp.dot(mine, r, preferred_element_type=f32) for r in right]
    upper = lax.broadcasted_iota(jnp.int32, (8, 128), 0) < 4
    xs = []
    for d in range(4):
        h0, h1 = (
            lanes([p[d * 8 : d * 8 + 8, h * 128 + d * 32 : h * 128 + d * 32 + 32] for p in prods])
            for h in range(2)
        )
        xs.append(jnp.where(upper, h0, h1))
    x = jnp.swapaxes(jnp.stack(xs + xs, axis=0), 0, 1)
    x = [jnp.where(upper, x[i], x[4 + i]).astype(bf16) for i in range(4)]
    lane = lax.broadcasted_iota(jnp.int32, (512, 128), 0)
    col = lax.broadcasted_iota(jnp.int32, (512, 128), 1)
    pick = ((lane == here * 32 + col) & (col < 32)).astype(f32).astype(bf16)
    z1 = jnp.dot(z1_ref[...], pick, preferred_element_type=f32)
    n1 = jnp.dot(n1_ref[...], pick, preferred_element_type=f32).astype(bf16)
    same = jnp.dot(
        jnp.broadcast_to(same_ref[...], (8, 512)).astype(bf16), pick, preferred_element_type=f32
    )[0:1]
    gate = gates(n1, w_ref, 1, columns_of(w_ref)[:, 5:6], same)
    for q in range(4):
        zq, gq = (
            lanes([v[q * 32 + c * 8 : q * 32 + c * 8 + 8, 0:32] for c in range(4)]).astype(bf16)
            for v in (z1, gate)
        )
        for a in range(4):
            out_ref[a * 4 + q, 0:8, :] = x[a]
            out_ref[a * 4 + q, 8:16, :] = zq
            out_ref[a * 4 + q, 16:24, :] = gq


def last_kernel(got_ref, w_ref, out_ref, ys):
    x = jnp.swapaxes(got_ref[:, 0:8, :].astype(f32), 0, 1)
    x1 = jnp.concatenate([x[h * 4 + d] for d in range(4) for h in range(2)], axis=0)
    cols = columns_of(w_ref)
    xn = norm(x1, cols[:, 1:2], cols[:, 3:4])
    w = jnp.concatenate([w_ref[q, 352:384, :] for q in range(4)], axis=0)
    ys[...] = tn(w, xn)
    y = ys[pl.ds(pl.multiple_of(lax.axis_index("ch") * 32, 32), 32), :]
    home = lax.axis_index("x") * 4
    own = [got_ref[home + s].astype(f32) for s in range(4)]
    z1, gate = (
        jnp.concatenate(
            [lanes([o[r : r + 8, c * 32 : c * 32 + 32] for o in own]) for c in range(4)], axis=0
        )
        for r in (8, 16)
    )
    out = (z1 + gate * y).astype(bf16)
    out_ref[...] = nt(out, permutation()).astype(bf16)


def body(pair_rep, residue_mask, chain_ids, in_gain, in_bias, w_proj, w_gate, pair_bias, out_gain, out_bias, w_out):
    send = spread(pair_rep.reshape(32, 128))
    args = (
        residue_mask.reshape(1, 128),
        chain_ids.reshape(1, 128),
        in_gain,
        in_bias,
        pair_bias,
        out_gain,
        out_bias,
        w_proj.transpose(0, 2, 3, 1).reshape(256, 128),
        w_gate.transpose(0, 2, 1).reshape(64, 128),
        w_out.reshape(64, 128),
    )
    send, *args = lax.optimization_barrier((send, *args))
    got = lax.all_to_all(send, ("z", "ch"), 0, 0, tiled=True)
    packed, gains, pm, same = prepare(*args)
    packed = lax.all_gather(packed, "ch", axis=0)
    got, packed, gains, pm, same = lax.optimization_barrier((got, packed, gains, pm, same))
    send, z0, gate = call(
        first_kernel,
        [((32, 32, 128), bf16), ((128, 512), f32), ((128, 512), f32)],
        [got, gains, packed, pm, same],
    )
    got = lax.all_to_all(send, PLANE, 0, 0, tiled=True)
    (send,) = call(outgoing_kernel, [((32, 16, 128), bf16)], [got])
    got = lax.all_to_all(send, PLANE, 0, 0, tiled=True)
    send, z1, n1 = call(
        middle_kernel,
        [((32, 40, 128), bf16), ((128, 512), bf16), ((128, 512), bf16)],
        [got, z0, gate, gains, packed, pm],
    )
    got = lax.all_to_all(send, PLANE, 0, 0, tiled=True)
    (send,) = call(incoming_kernel, [((16, 24, 128), bf16)], [got, z1, n1, packed, same])
    got = lax.all_to_all(send, ("x", "ch"), 0, 0, tiled=True)
    (out,) = call(last_kernel, [((32, 128), bf16)], [got, packed], [(128, 128)])
    return out.reshape(32, 1, 128)


def solution(mesh):
    fine = Mesh(mesh.devices.reshape(4, 16, 2, 4), ("x", "z", "yh", "ch"))
    return jax.shard_map(
        body,
        mesh=fine,
        in_specs=(
            P("ch", ROW, None),
            P(),
            P(),
            P(),
            P(),
            P(None, None, None, "ch"),
            P(None, None, "ch"),
            P(None, "ch"),
            P(None, "ch"),
            P(None, "ch"),
            P(None, "ch", None),
        ),
        out_specs=P("ch", ROW, None),
        check_vma=False,
    )
```

```python
import jax
import jax.numpy as jnp
from jax import lax
from jax.experimental import pallas as pl
from jax.experimental.pallas import tpu as pltpu
from jax.sharding import Mesh, PartitionSpec as P

epsilon = 1e-05
bf16 = jnp.bfloat16
f32 = jnp.float32
ROW = ("x", "z", "yh")
PLANE = ("x", "yh", "ch")
VMEM = pl.BlockSpec(memory_space=pltpu.VMEM)
HBM = pl.BlockSpec(memory_space=pltpu.HBM)


def call(kernel, outs, ins, scratch=(), flops=100_000_000):
    moved = sum(a.size * a.dtype.itemsize for a in ins)
    return pl.pallas_call(
        kernel,
        out_shape=[jax.ShapeDtypeStruct(s, d) for s, d in outs],
        in_specs=[VMEM] * len(ins),
        out_specs=[VMEM] * len(outs),
        scratch_shapes=[pltpu.VMEM(s, f32) for s in scratch],
        compiler_params=pltpu.CompilerParams(vmem_limit_bytes=32 * 1024 * 1024),
        cost_estimate=pl.CostEstimate(flops=flops, bytes_accessed=moved, transcendentals=0),
    )(*ins)


def nt(a, b):
    return lax.dot_general(a, b, (((1,), (1,)), ((), ())), preferred_element_type=f32)


def sigmoid(v):
    return 0.5 * jnp.tanh(0.5 * v) + 0.5


def norm(v, gain, bias):
    mean = jnp.mean(v, axis=0, keepdims=True)
    var = jnp.mean(v * v, axis=0, keepdims=True) - mean * mean
    return ((v - mean) * lax.rsqrt(var + epsilon) * gain + bias).astype(bf16)


def lanes(pieces):
    return jnp.concatenate(pieces, axis=1)


def permutation(k_dim=0):
    k = lax.broadcasted_iota(jnp.int32, (128, 128), k_dim)
    p = lax.broadcasted_iota(jnp.int32, (128, 128), 1 - k_dim)
    place = (k & 96) | ((k & 1) << 4) | ((k & 31) >> 1)
    return (place == p).astype(f32).astype(bf16)


def spread_kernel(x_ref, out_ref, tile, sems):
    t = jnp.dot(x_ref[...], permutation(), preferred_element_type=f32)
    for q in range(4):
        piece = lanes([t[c * 8 : c * 8 + 8, q * 32 : q * 32 + 32] for c in range(4)])
        tile[q] = piece.astype(bf16)
    copies = [pltpu.make_async_copy(tile, out_ref.at[z * 4 : z * 4 + 4], sems.at[z]) for z in range(16)]
    for c in copies:
        c.start()
    for c in copies:
        c.wait()


def spread(x):
    return pl.pallas_call(
        spread_kernel,
        out_shape=jax.ShapeDtypeStruct((64, 8, 128), bf16),
        in_specs=[VMEM],
        out_specs=HBM,
        scratch_shapes=[pltpu.VMEM((4, 8, 128), bf16), pltpu.SemaphoreType.DMA((16,))],
        compiler_params=pltpu.CompilerParams(vmem_limit_bytes=32 * 1024 * 1024),
    )(x)


def prepare_kernel(
    mask_ref, chain_ref, gain_ref, bias_ref, pb_ref, og_ref, ob_ref, wp_ref, wg_ref, wo_ref,
    packed_ref, gains_ref, pm_ref, same_ref, marks, inner, outer, sems,
):
    places = [
        (wp_ref, packed_ref.at[0:256]),
        (wg_ref, packed_ref.at[256:320]),
        (wo_ref, packed_ref.at[320:384]),
        (mask_ref, marks.at[0:1]),
        (chain_ref, marks.at[1:2]),
        (gain_ref, inner.at[0:2]),
        (bias_ref, inner.at[2:4]),
        (og_ref, outer.at[0]),
        (ob_ref, outer.at[1]),
        (pb_ref, outer.at[2]),
    ]
    copies = [pltpu.make_async_copy(a, b, sems.at[i]) for i, (a, b) in enumerate(places)]
    for c in copies[3:] + copies[:3]:
        c.start()
    ix, iyh, q = (lax.axis_index(a) for a in ("x", "yh", "ch"))
    place = lax.broadcasted_iota(jnp.int32, (128, 512), 0)
    pair = lax.broadcasted_iota(jnp.int32, (128, 512), 1)
    rows = place == (ix * 32 + iyh) + ((pair >> 5) << 1)
    columns = place == q * 32 + (((pair & 15) << 1) | ((pair >> 4) & 1))
    rows, columns = (v.astype(f32).astype(bf16) for v in (rows, columns))
    for c in copies[3:]:
        c.wait()
    m = marks[0:2, :].astype(f32)
    m = jnp.concatenate([m, jnp.zeros((6, 128), f32)], axis=0).astype(bf16)
    r = jnp.dot(m, rows, preferred_element_type=f32)
    c = jnp.dot(m, columns, preferred_element_type=f32)
    pm_ref[...] = r[0:1] * c[0:1]
    same_ref[...] = (r[1:2] == c[1:2]).astype(f32)
    g = jnp.concatenate([inner[0:4, :], jnp.zeros((124, 128), f32)], axis=0)
    gains_ref[...] = g.T[:, 0:8]
    v = jnp.concatenate([outer[i] for i in range(3)], axis=0)
    hi = v.astype(bf16).astype(f32)
    mid = (v - hi).astype(bf16).astype(f32)
    low = v - hi - mid
    v = jnp.concatenate([hi, mid, low, jnp.zeros((110, 32), f32)], axis=0)
    v = lanes([v, jnp.zeros((128, 96), f32)])
    packed_ref[384:416, :] = v.T[0:32].astype(bf16)
    for c in copies[:3]:
        c.wait()


def prepare(*args):
    return pl.pallas_call(
        prepare_kernel,
        out_shape=[
            jax.ShapeDtypeStruct((416, 128), bf16),
            jax.ShapeDtypeStruct((128, 8), f32),
            jax.ShapeDtypeStruct((1, 512), f32),
            jax.ShapeDtypeStruct((1, 512), f32),
        ],
        in_specs=[HBM] * 10,
        out_specs=[VMEM] * 4,
        scratch_shapes=[
            pltpu.VMEM((2, 128), jnp.int32),
            pltpu.VMEM((4, 128), f32),
            pltpu.VMEM((3, 2, 32), f32),
            pltpu.SemaphoreType.DMA((10,)),
        ],
        compiler_params=pltpu.CompilerParams(vmem_limit_bytes=32 * 1024 * 1024),
    )(*args)


def arrange_kernel(w_ref, cols_ref, wo_ref, own_ref, back_ref, scr):
    v = jnp.concatenate([w_ref[q, 384:416, :].astype(f32) for q in range(4)], axis=0)
    cols_ref[...] = v[:, 0:8] + v[:, 6:14] + v[:, 12:20]
    for u in range(2):
        w = jnp.concatenate([w_ref[q, 320 + u * 32 : 352 + u * 32, :] for q in range(4)], axis=0)
        w = w.astype(f32).T
        if u == 0:
            wo_ref[...] = w.astype(bf16)
        else:
            scr[...] = w
    own = pl.multiple_of(lax.axis_index("ch") * 32, 32)
    own_ref[...] = scr[pl.ds(own, 32), :].astype(bf16)
    back_ref[...] = permutation(1)


def project(n, w_ref, u, pm):
    sides = ([], [])
    for q in range(4):
        w = w_ref[q, u * 128 : u * 128 + 128, :]
        p = jnp.dot(w, n, preferred_element_type=f32)
        sides[0].append(sigmoid(p[0:32]) * p[32:64] * pm)
        sides[1].append(sigmoid(p[64:96]) * p[96:128] * pm)
    return sides


def slabs(v):
    return [lanes([a[:, z * 32 : z * 32 + 32] for a in v]) for z in range(16)]


def gates(n, w_ref, u, cols, same):
    w = jnp.concatenate([w_ref[q, 256 + u * 32 : 288 + u * 32, :] for q in range(4)], axis=0)
    return sigmoid(jnp.dot(w, n, preferred_element_type=f32) + cols * same)


def first_kernel(got_ref, gain_ref, cols_ref, w_ref, pm_ref, same_ref, out_ref, z_ref, gate_ref):
    rows = []
    for q in range(4):
        for c in range(4):
            pieces = [got_ref[z * 4 + q].astype(f32)[:, c * 32 : c * 32 + 32] for z in range(16)]
            rows.append(lanes(pieces))
    z0 = jnp.concatenate(rows, axis=0)
    z_ref[...] = z0
    n = norm(z0, gain_ref[:, 0:1], gain_ref[:, 2:3])
    gate_ref[...] = gates(n, w_ref, 0, cols_ref[:, 4:5], same_ref[...])
    for s, v in enumerate(project(n, w_ref, 0, pm_ref[...])):
        v = jnp.swapaxes(jnp.stack(slabs(v), axis=0), 0, 1)
        out_ref[:, s * 16 : s * 16 + 16, :] = v.astype(bf16)


def outgoing_kernel(got_ref, out_ref):
    row = lax.broadcasted_iota(jnp.int32, (128, 512), 0) >> 5
    lane = (lax.broadcasted_iota(jnp.int32, (128, 512), 1) >> 5) & 3
    same = row == lane
    left, right = [], []
    for q in range(4):
        left.append(jnp.concatenate([got_ref[a * 4 + q, 0:16, :] for a in range(8)], axis=0))
        right.append(jnp.concatenate([got_ref[a * 4 + q, 16:32, :] for a in range(8)], axis=0))
    left, right = lanes(left), lanes(right)
    for q in range(4):
        part = right[q * 32 : q * 32 + 32].astype(f32)
        block = jnp.where(same, jnp.concatenate([part] * 4, axis=0), 0.0).astype(bf16)
        x = nt(left, block).astype(bf16)
        for b in range(8):
            out_ref[b * 4 + q] = x[b * 16 : b * 16 + 16]


def middle_kernel(got_ref, z_ref, gate_ref, gain_ref, cols_ref, wo_ref, w_ref, pm_ref, out_ref, z1_ref, n1_ref):
    x = jnp.swapaxes(got_ref[...].astype(f32), 0, 1)
    x0 = jnp.concatenate(
        [lanes([x[z][:, d * 32 : d * 32 + 32] for z in range(16)]) for d in range(4)], axis=0
    )
    xn = norm(x0, cols_ref[:, 0:1], cols_ref[:, 2:3])
    y = jnp.dot(wo_ref[...], xn, preferred_element_type=f32)
    z1 = (z_ref[...] + gate_ref[...] * y).astype(bf16)
    z1_ref[...] = z1
    n1 = norm(z1.astype(f32), gain_ref[:, 1:2], gain_ref[:, 3:4])
    n1_ref[...] = n1
    left, right = project(n1, w_ref, 1, pm_ref[...])
    lane = lax.broadcasted_iota(jnp.int32, (512, 128), 0)
    col = lax.broadcasted_iota(jnp.int32, (512, 128), 1)
    want = ((col & 15) << 5) | (((col >> 4) & 1) << 4) | lax.axis_index("z")
    pick = ((lane == want) & (col < 32)).astype(f32).astype(bf16)
    left = lanes([jnp.dot(v.astype(bf16), pick, preferred_element_type=f32)[:, 0:32] for v in left])
    v = jnp.swapaxes(jnp.stack(slabs(right) + [left] * 8, axis=0), 0, 1)
    first = lax.broadcasted_iota(jnp.int32, (8, 128), 0) == 0
    for g in range(16):
        marks = jnp.where(first, v[g, 16:24], v[16 + g, 16:24]).astype(bf16)
        for yh in range(2):
            at = (g // 4) * 8 + yh * 4 + g % 4
            out_ref[at, 0:16, :] = v[g, 0:16].astype(bf16)
            out_ref[at, 16:32, :] = v[16 + g, 0:16].astype(bf16)
            out_ref[at, 32:40, :] = marks


def incoming_kernel(got_ref, z1_ref, n1_ref, cols_ref, w_ref, same_ref, out_ref):
    here = lax.axis_index("z")
    right = [
        lanes(
            [
                jnp.concatenate([got_ref[a * 4 + q, h * 16 : h * 16 + 16, :] for a in range(8)], axis=0)
                for h in range(2)
            ]
        )
        for q in range(4)
    ]
    row = lax.broadcasted_iota(jnp.int32, (32, 128), 0)
    lane = lax.broadcasted_iota(jnp.int32, (32, 128), 1)
    wanted = ((row >> 3) == (lane >> 5)) & (((lane >> 4) & 1) == lax.axis_index("yh"))
    parts = []
    for a in range(8):
        tiles = [got_ref[a * 4 + x, 32:40, :].astype(f32) for x in range(4)]
        rows = jnp.concatenate([t[h : h + 1] for h in range(2) for t in tiles], axis=0)
        parts.append(jnp.where(wanted, jnp.concatenate([rows] * 4, axis=0), 0.0).astype(bf16))
    source = lax.broadcasted_iota(jnp.int32, (1024, 128), 0)
    target = lax.broadcasted_iota(jnp.int32, (1024, 128), 1)
    place = ((source >> 7) << 4) | (source & 15)
    place = (place == target).astype(f32).astype(bf16)
    mine = jnp.dot(lanes(parts), place, preferred_element_type=f32).astype(bf16)
    prods = [jnp.dot(mine, r, preferred_element_type=f32) for r in right]
    upper = lax.broadcasted_iota(jnp.int32, (8, 128), 0) < 4
    xs = []
    for d in range(4):
        h0, h1 = (
            lanes([p[d * 8 : d * 8 + 8, h * 128 + d * 32 : h * 128 + d * 32 + 32] for p in prods])
            for h in range(2)
        )
        xs.append(jnp.where(upper, h0, h1))
    x = jnp.swapaxes(jnp.stack(xs + xs, axis=0), 0, 1)
    x = [jnp.where(upper, x[i], x[4 + i]).astype(bf16) for i in range(4)]
    lane = lax.broadcasted_iota(jnp.int32, (512, 128), 0)
    col = lax.broadcasted_iota(jnp.int32, (512, 128), 1)
    pick = ((lane == here * 32 + col) & (col < 32)).astype(f32).astype(bf16)
    z1 = jnp.dot(z1_ref[...], pick, preferred_element_type=f32)
    n1 = jnp.dot(n1_ref[...], pick, preferred_element_type=f32).astype(bf16)
    same = jnp.dot(
        jnp.broadcast_to(same_ref[...], (8, 512)).astype(bf16), pick, preferred_element_type=f32
    )[0:1]
    gate = gates(n1, w_ref, 1, cols_ref[:, 5:6], same)
    for q in range(4):
        zq, gq = (
            lanes([v[q * 32 + c * 8 : q * 32 + c * 8 + 8, 0:32] for c in range(4)]).astype(bf16)
            for v in (z1, gate)
        )
        for a in range(4):
            out_ref[a * 4 + q, 0:8, :] = x[a]
            out_ref[a * 4 + q, 8:16, :] = zq
            out_ref[a * 4 + q, 16:24, :] = gq


def last_kernel(got_ref, cols_ref, own_ref, back_ref, out_ref):
    x = jnp.swapaxes(got_ref[:, 0:8, :].astype(f32), 0, 1)
    x1 = jnp.concatenate([x[h * 4 + d] for d in range(4) for h in range(2)], axis=0)
    xn = norm(x1, cols_ref[:, 1:2], cols_ref[:, 3:4])
    y = jnp.dot(own_ref[...], xn, preferred_element_type=f32)
    home = lax.axis_index("x") * 4
    own = [got_ref[home + s].astype(f32) for s in range(4)]
    z1, gate = (
        jnp.concatenate(
            [lanes([o[r : r + 8, c * 32 : c * 32 + 32] for o in own]) for c in range(4)], axis=0
        )
        for r in (8, 16)
    )
    out = (z1 + gate * y).astype(bf16)
    out_ref[...] = jnp.dot(out, back_ref[...], preferred_element_type=f32).astype(bf16)


def body(pair_rep, residue_mask, chain_ids, in_gain, in_bias, w_proj, w_gate, pair_bias, out_gain, out_bias, w_out):
    send = spread(pair_rep.reshape(32, 128))
    args = (
        residue_mask.reshape(1, 128),
        chain_ids.reshape(1, 128),
        in_gain,
        in_bias,
        pair_bias,
        out_gain,
        out_bias,
        w_proj.transpose(0, 2, 3, 1).reshape(256, 128),
        w_gate.transpose(0, 2, 1).reshape(64, 128),
        w_out.reshape(64, 128),
    )
    send, *args = lax.optimization_barrier((send, *args))
    got = lax.all_to_all(send, ("z", "ch"), 0, 0, tiled=True)
    packed, gains, pm, same = prepare(*args)
    packed = lax.all_gather(packed, "ch", axis=0)
    cols, wo, own, back = call(
        arrange_kernel,
        [((128, 8), f32), ((128, 128), bf16), ((32, 128), bf16), ((128, 128), bf16)],
        [packed],
        [(128, 128)],
        flops=1_000_000,
    )
    got, packed, gains, pm, same, cols, wo, own, back = lax.optimization_barrier(
        (got, packed, gains, pm, same, cols, wo, own, back)
    )
    send, z0, gate = call(
        first_kernel,
        [((32, 32, 128), bf16), ((128, 512), f32), ((128, 512), f32)],
        [got, gains, cols, packed, pm, same],
    )
    got = lax.all_to_all(send, PLANE, 0, 0, tiled=True)
    (send,) = call(outgoing_kernel, [((32, 16, 128), bf16)], [got])
    got = lax.all_to_all(send, PLANE, 0, 0, tiled=True)
    send, z1, n1 = call(
        middle_kernel,
        [((32, 40, 128), bf16), ((128, 512), bf16), ((128, 512), bf16)],
        [got, z0, gate, gains, cols, wo, packed, pm],
    )
    got = lax.all_to_all(send, PLANE, 0, 0, tiled=True)
    (send,) = call(incoming_kernel, [((16, 24, 128), bf16)], [got, z1, n1, cols, packed, same])
    got = lax.all_to_all(send, ("x", "ch"), 0, 0, tiled=True)
    (out,) = call(last_kernel, [((32, 128), bf16)], [got, cols, own, back])
    return out.reshape(32, 1, 128)


def solution(mesh):
    fine = Mesh(mesh.devices.reshape(4, 16, 2, 4), ("x", "z", "yh", "ch"))
    return jax.shard_map(
        body,
        mesh=fine,
        in_specs=(
            P("ch", ROW, None),
            P(),
            P(),
            P(),
            P(),
            P(None, None, None, "ch"),
            P(None, None, "ch"),
            P(None, "ch"),
            P(None, "ch"),
            P(None, "ch"),
            P(None, "ch", None),
        ),
        out_specs=P("ch", ROW, None),
        check_vma=False,
    )
```

```python
import jax
import jax.numpy as jnp
from jax import lax
from jax.experimental import pallas as pl
from jax.experimental.pallas import tpu as pltpu
from jax.sharding import Mesh, PartitionSpec as P

epsilon = 1e-05
bf16 = jnp.bfloat16
f32 = jnp.float32
ROW = ("x", "z", "yh")
PLANE = ("x", "yh", "ch")
ALL = ("x", "z", "yh", "ch")
FIRST_Z = 8
COLUMNS = [
    [((x * 16 + (z + FIRST_Z) % 16) * 2 + yh) * 4 + q for z in range(16) for q in range(4)]
    for x in range(4)
    for yh in range(2)
]
VMEM = pl.BlockSpec(memory_space=pltpu.VMEM)
HBM = pl.BlockSpec(memory_space=pltpu.HBM)


def call(kernel, outs, ins, scratch=(), flops=100_000_000):
    moved = sum(a.size * a.dtype.itemsize for a in ins)
    return pl.pallas_call(
        kernel,
        out_shape=[jax.ShapeDtypeStruct(s, d) for s, d in outs],
        in_specs=[VMEM] * len(ins),
        out_specs=[VMEM] * len(outs),
        scratch_shapes=[pltpu.VMEM(s, f32) for s in scratch],
        compiler_params=pltpu.CompilerParams(vmem_limit_bytes=32 * 1024 * 1024),
        cost_estimate=pl.CostEstimate(flops=flops, bytes_accessed=moved, transcendentals=0),
    )(*ins)


def nt(a, b):
    return lax.dot_general(a, b, (((1,), (1,)), ((), ())), preferred_element_type=f32)


def sigmoid(v):
    return 0.5 * jnp.tanh(0.5 * v) + 0.5


def norm(v, gain, bias):
    mean = jnp.mean(v, axis=0, keepdims=True)
    var = jnp.mean(v * v, axis=0, keepdims=True) - mean * mean
    return ((v - mean) * lax.rsqrt(var + epsilon) * gain + bias).astype(bf16)


def lanes(pieces):
    return jnp.concatenate(pieces, axis=1)


def permutation(k_dim=0):
    k = lax.broadcasted_iota(jnp.int32, (128, 128), k_dim)
    p = lax.broadcasted_iota(jnp.int32, (128, 128), 1 - k_dim)
    place = (k & 96) | ((k & 1) << 4) | ((k & 31) >> 1)
    return (place == p).astype(f32).astype(bf16)


def spread_kernel(x_ref, out_ref, tile, sems):
    t = jnp.dot(x_ref[...], permutation(), preferred_element_type=f32)
    for q in range(4):
        piece = lanes([t[c * 8 : c * 8 + 8, q * 32 : q * 32 + 32] for c in range(4)])
        tile[q] = piece.astype(bf16)
    copies = [pltpu.make_async_copy(tile, out_ref.at[z * 4 : z * 4 + 4], sems.at[z]) for z in range(16)]
    for c in copies:
        c.start()
    for c in copies:
        c.wait()


def spread(x):
    return pl.pallas_call(
        spread_kernel,
        out_shape=jax.ShapeDtypeStruct((64, 8, 128), bf16),
        in_specs=[VMEM],
        out_specs=HBM,
        scratch_shapes=[pltpu.VMEM((4, 8, 128), bf16), pltpu.SemaphoreType.DMA((16,))],
        compiler_params=pltpu.CompilerParams(vmem_limit_bytes=32 * 1024 * 1024),
    )(x)


def prepare_kernel(
    mask_ref, chain_ref, gain_ref, bias_ref, pb_ref, og_ref, ob_ref, wp_ref, wg_ref, wo_ref,
    packed_ref, gains_ref, pm_ref, same_ref, marks, inner, outer, sems,
):
    places = [
        (wp_ref, packed_ref.at[0:256]),
        (wg_ref, packed_ref.at[256:320]),
        (wo_ref, packed_ref.at[320:384]),
        (mask_ref, marks.at[0:1]),
        (chain_ref, marks.at[1:2]),
        (gain_ref, inner.at[0:2]),
        (bias_ref, inner.at[2:4]),
        (og_ref, outer.at[0]),
        (ob_ref, outer.at[1]),
        (pb_ref, outer.at[2]),
    ]
    copies = [pltpu.make_async_copy(a, b, sems.at[i]) for i, (a, b) in enumerate(places)]
    for c in copies[3:] + copies[:3]:
        c.start()
    ix, iyh, q = (lax.axis_index(a) for a in ("x", "yh", "ch"))
    place = lax.broadcasted_iota(jnp.int32, (128, 512), 0)
    pair = lax.broadcasted_iota(jnp.int32, (128, 512), 1)
    rows = place == (ix * 32 + iyh) + ((pair >> 5) << 1)
    columns = place == q * 32 + (((pair & 15) << 1) | ((pair >> 4) & 1))
    rows, columns = (v.astype(f32).astype(bf16) for v in (rows, columns))
    for c in copies[3:]:
        c.wait()
    m = marks[0:2, :].astype(f32)
    m = jnp.concatenate([m, jnp.zeros((6, 128), f32)], axis=0).astype(bf16)
    r = jnp.dot(m, rows, preferred_element_type=f32)
    c = jnp.dot(m, columns, preferred_element_type=f32)
    pm_ref[...] = r[0:1] * c[0:1]
    same_ref[...] = (r[1:2] == c[1:2]).astype(f32)
    g = jnp.concatenate([inner[0:4, :], jnp.zeros((124, 128), f32)], axis=0)
    gains_ref[...] = g.T[:, 0:8]
    v = jnp.concatenate([outer[i] for i in range(3)], axis=0)
    hi = v.astype(bf16).astype(f32)
    mid = (v - hi).astype(bf16).astype(f32)
    low = v - hi - mid
    v = jnp.concatenate([hi, mid, low, jnp.zeros((110, 32), f32)], axis=0)
    v = lanes([v, jnp.zeros((128, 96), f32)])
    packed_ref[384:416, :] = v.T[0:32].astype(bf16)
    for c in copies[:3]:
        c.wait()


def prepare(*args):
    return pl.pallas_call(
        prepare_kernel,
        out_shape=[
            jax.ShapeDtypeStruct((416, 128), bf16),
            jax.ShapeDtypeStruct((128, 8), f32),
            jax.ShapeDtypeStruct((1, 512), f32),
            jax.ShapeDtypeStruct((1, 512), f32),
        ],
        in_specs=[HBM] * 10,
        out_specs=[VMEM] * 4,
        scratch_shapes=[
            pltpu.VMEM((2, 128), jnp.int32),
            pltpu.VMEM((4, 128), f32),
            pltpu.VMEM((3, 2, 32), f32),
            pltpu.SemaphoreType.DMA((10,)),
        ],
        compiler_params=pltpu.CompilerParams(vmem_limit_bytes=32 * 1024 * 1024),
    )(*args)


def arrange_kernel(w_ref, cols_ref, wo_ref, own_ref, back_ref, scr):
    v = jnp.concatenate([w_ref[q, 384:416, :].astype(f32) for q in range(4)], axis=0)
    cols_ref[...] = v[:, 0:8] + v[:, 6:14] + v[:, 12:20]
    for u in range(2):
        w = jnp.concatenate([w_ref[q, 320 + u * 32 : 352 + u * 32, :] for q in range(4)], axis=0)
        w = w.astype(f32).T
        if u == 0:
            wo_ref[...] = w.astype(bf16)
        else:
            scr[...] = w
    own = pl.multiple_of(lax.axis_index("ch") * 32, 32)
    own_ref[...] = scr[pl.ds(own, 32), :].astype(bf16)
    back_ref[...] = permutation(1)


def project(n, w_ref, u, pm):
    sides = ([], [])
    for q in range(4):
        w = w_ref[q, u * 128 : u * 128 + 128, :]
        p = jnp.dot(w, n, preferred_element_type=f32)
        sides[0].append(sigmoid(p[0:32]) * p[32:64] * pm)
        sides[1].append(sigmoid(p[64:96]) * p[96:128] * pm)
    return sides


def slabs(v):
    return [lanes([a[:, z * 32 : z * 32 + 32] for a in v]) for z in range(16)]


def gates(n, w_ref, u, cols, same):
    w = jnp.concatenate([w_ref[q, 256 + u * 32 : 288 + u * 32, :] for q in range(4)], axis=0)
    return sigmoid(jnp.dot(w, n, preferred_element_type=f32) + cols * same)


def first_kernel(got_ref, gain_ref, cols_ref, w_ref, pm_ref, same_ref, out_ref, z_ref, gate_ref):
    rows = []
    for q in range(4):
        for c in range(4):
            pieces = [
                got_ref[(z - FIRST_Z) % 16 * 4 + q].astype(f32)[:, c * 32 : c * 32 + 32] for z in range(16)
            ]
            rows.append(lanes(pieces))
    z0 = jnp.concatenate(rows, axis=0)
    z_ref[...] = z0
    n = norm(z0, gain_ref[:, 0:1], gain_ref[:, 2:3])
    gate_ref[...] = gates(n, w_ref, 0, cols_ref[:, 4:5], same_ref[...])
    for s, v in enumerate(project(n, w_ref, 0, pm_ref[...])):
        v = jnp.swapaxes(jnp.stack(slabs(v), axis=0), 0, 1)
        out_ref[:, s * 16 : s * 16 + 16, :] = v.astype(bf16)


def outgoing_kernel(got_ref, out_ref):
    row = lax.broadcasted_iota(jnp.int32, (128, 512), 0) >> 5
    lane = (lax.broadcasted_iota(jnp.int32, (128, 512), 1) >> 5) & 3
    same = row == lane
    left, right = [], []
    for q in range(4):
        left.append(jnp.concatenate([got_ref[a * 4 + q, 0:16, :] for a in range(8)], axis=0))
        right.append(jnp.concatenate([got_ref[a * 4 + q, 16:32, :] for a in range(8)], axis=0))
    left, right = lanes(left), lanes(right)
    for q in range(4):
        part = right[q * 32 : q * 32 + 32].astype(f32)
        block = jnp.where(same, jnp.concatenate([part] * 4, axis=0), 0.0).astype(bf16)
        x = nt(left, block).astype(bf16)
        for b in range(8):
            out_ref[b * 4 + q] = x[b * 16 : b * 16 + 16]


def middle_kernel(got_ref, z_ref, gate_ref, gain_ref, cols_ref, wo_ref, w_ref, pm_ref, out_ref, z1_ref, n1_ref):
    x = jnp.swapaxes(got_ref[...].astype(f32), 0, 1)
    x0 = jnp.concatenate(
        [lanes([x[z][:, d * 32 : d * 32 + 32] for z in range(16)]) for d in range(4)], axis=0
    )
    xn = norm(x0, cols_ref[:, 0:1], cols_ref[:, 2:3])
    y = jnp.dot(wo_ref[...], xn, preferred_element_type=f32)
    z1 = (z_ref[...] + gate_ref[...] * y).astype(bf16)
    z1_ref[...] = z1
    n1 = norm(z1.astype(f32), gain_ref[:, 1:2], gain_ref[:, 3:4])
    n1_ref[...] = n1
    left, right = project(n1, w_ref, 1, pm_ref[...])
    lane = lax.broadcasted_iota(jnp.int32, (512, 128), 0)
    col = lax.broadcasted_iota(jnp.int32, (512, 128), 1)
    want = ((col & 15) << 5) | (((col >> 4) & 1) << 4) | lax.axis_index("z")
    pick = ((lane == want) & (col < 32)).astype(f32).astype(bf16)
    left = lanes([jnp.dot(v.astype(bf16), pick, preferred_element_type=f32)[:, 0:32] for v in left])
    v = jnp.swapaxes(jnp.stack(slabs(right) + [left] * 8, axis=0), 0, 1)
    first = lax.broadcasted_iota(jnp.int32, (8, 128), 0) == 0
    for g in range(16):
        marks = jnp.where(first, v[g, 16:24], v[16 + g, 16:24]).astype(bf16)
        for yh in range(2):
            at = (g // 4) * 8 + yh * 4 + g % 4
            out_ref[at, 0:16, :] = v[g, 0:16].astype(bf16)
            out_ref[at, 16:32, :] = v[16 + g, 0:16].astype(bf16)
            out_ref[at, 32:40, :] = marks


def incoming_kernel(got_ref, z1_ref, n1_ref, cols_ref, w_ref, same_ref, out_ref):
    here = lax.axis_index("z")
    right = [
        lanes(
            [
                jnp.concatenate([got_ref[a * 4 + q, h * 16 : h * 16 + 16, :] for a in range(8)], axis=0)
                for h in range(2)
            ]
        )
        for q in range(4)
    ]
    row = lax.broadcasted_iota(jnp.int32, (32, 128), 0)
    lane = lax.broadcasted_iota(jnp.int32, (32, 128), 1)
    wanted = ((row >> 3) == (lane >> 5)) & (((lane >> 4) & 1) == lax.axis_index("yh"))
    parts = []
    for a in range(8):
        tiles = [got_ref[a * 4 + x, 32:40, :].astype(f32) for x in range(4)]
        rows = jnp.concatenate([t[h : h + 1] for h in range(2) for t in tiles], axis=0)
        parts.append(jnp.where(wanted, jnp.concatenate([rows] * 4, axis=0), 0.0).astype(bf16))
    source = lax.broadcasted_iota(jnp.int32, (1024, 128), 0)
    target = lax.broadcasted_iota(jnp.int32, (1024, 128), 1)
    place = ((source >> 7) << 4) | (source & 15)
    place = (place == target).astype(f32).astype(bf16)
    mine = jnp.dot(lanes(parts), place, preferred_element_type=f32).astype(bf16)
    prods = [jnp.dot(mine, r, preferred_element_type=f32) for r in right]
    upper = lax.broadcasted_iota(jnp.int32, (8, 128), 0) < 4
    xs = []
    for d in range(4):
        h0, h1 = (
            lanes([p[d * 8 : d * 8 + 8, h * 128 + d * 32 : h * 128 + d * 32 + 32] for p in prods])
            for h in range(2)
        )
        xs.append(jnp.where(upper, h0, h1))
    x = jnp.swapaxes(jnp.stack(xs + xs, axis=0), 0, 1)
    x = [jnp.where(upper, x[i], x[4 + i]).astype(bf16) for i in range(4)]
    lane = lax.broadcasted_iota(jnp.int32, (512, 128), 0)
    col = lax.broadcasted_iota(jnp.int32, (512, 128), 1)
    pick = ((lane == here * 32 + col) & (col < 32)).astype(f32).astype(bf16)
    z1 = jnp.dot(z1_ref[...], pick, preferred_element_type=f32)
    n1 = jnp.dot(n1_ref[...], pick, preferred_element_type=f32).astype(bf16)
    same = jnp.dot(
        jnp.broadcast_to(same_ref[...], (8, 512)).astype(bf16), pick, preferred_element_type=f32
    )[0:1]
    gate = gates(n1, w_ref, 1, cols_ref[:, 5:6], same)
    for q in range(4):
        zq, gq = (
            lanes([v[q * 32 + c * 8 : q * 32 + c * 8 + 8, 0:32] for c in range(4)]).astype(bf16)
            for v in (z1, gate)
        )
        for a in range(4):
            out_ref[a * 4 + q, 0:8, :] = x[a]
            out_ref[a * 4 + q, 8:16, :] = zq
            out_ref[a * 4 + q, 16:24, :] = gq


def last_kernel(got_ref, cols_ref, own_ref, back_ref, out_ref):
    x = jnp.swapaxes(got_ref[:, 0:8, :].astype(f32), 0, 1)
    x1 = jnp.concatenate([x[h * 4 + d] for d in range(4) for h in range(2)], axis=0)
    xn = norm(x1, cols_ref[:, 1:2], cols_ref[:, 3:4])
    y = jnp.dot(own_ref[...], xn, preferred_element_type=f32)
    home = lax.axis_index("x") * 4
    own = [got_ref[home + s].astype(f32) for s in range(4)]
    z1, gate = (
        jnp.concatenate(
            [lanes([o[r : r + 8, c * 32 : c * 32 + 32] for o in own]) for c in range(4)], axis=0
        )
        for r in (8, 16)
    )
    out = (z1 + gate * y).astype(bf16)
    out_ref[...] = jnp.dot(out, back_ref[...], preferred_element_type=f32).astype(bf16)


def body(pair_rep, residue_mask, chain_ids, in_gain, in_bias, w_proj, w_gate, pair_bias, out_gain, out_bias, w_out):
    send = spread(pair_rep.reshape(32, 128))
    args = (
        residue_mask.reshape(1, 128),
        chain_ids.reshape(1, 128),
        in_gain,
        in_bias,
        pair_bias,
        out_gain,
        out_bias,
        w_proj.transpose(0, 2, 3, 1).reshape(256, 128),
        w_gate.transpose(0, 2, 1).reshape(64, 128),
        w_out.reshape(64, 128),
    )
    send, *args = lax.optimization_barrier((send, *args))
    got = lax.all_to_all(send, ALL, 0, 0, axis_index_groups=COLUMNS, tiled=True)
    packed, gains, pm, same = prepare(*args)
    packed = lax.all_gather(packed, "ch", axis=0)
    cols, wo, own, back = call(
        arrange_kernel,
        [((128, 8), f32), ((128, 128), bf16), ((32, 128), bf16), ((128, 128), bf16)],
        [packed],
        [(128, 128)],
        flops=1_000_000,
    )
    got, packed, gains, pm, same, cols, wo, own, back = lax.optimization_barrier(
        (got, packed, gains, pm, same, cols, wo, own, back)
    )
    send, z0, gate = call(
        first_kernel,
        [((32, 32, 128), bf16), ((128, 512), f32), ((128, 512), f32)],
        [got, gains, cols, packed, pm, same],
    )
    got = lax.all_to_all(send, PLANE, 0, 0, tiled=True)
    (send,) = call(outgoing_kernel, [((32, 16, 128), bf16)], [got])
    got = lax.all_to_all(send, PLANE, 0, 0, tiled=True)
    send, z1, n1 = call(
        middle_kernel,
        [((32, 40, 128), bf16), ((128, 512), bf16), ((128, 512), bf16)],
        [got, z0, gate, gains, cols, wo, packed, pm],
    )
    got = lax.all_to_all(send, PLANE, 0, 0, tiled=True)
    (send,) = call(incoming_kernel, [((16, 24, 128), bf16)], [got, z1, n1, cols, packed, same])
    got = lax.all_to_all(send, ("x", "ch"), 0, 0, tiled=True)
    (out,) = call(last_kernel, [((32, 128), bf16)], [got, cols, own, back])
    return out.reshape(32, 1, 128)


def solution(mesh):
    fine = Mesh(mesh.devices.reshape(4, 16, 2, 4), ("x", "z", "yh", "ch"))
    return jax.shard_map(
        body,
        mesh=fine,
        in_specs=(
            P("ch", ROW, None),
            P(),
            P(),
            P(),
            P(),
            P(None, None, None, "ch"),
            P(None, None, "ch"),
            P(None, "ch"),
            P(None, "ch"),
            P(None, "ch"),
            P(None, "ch", None),
        ),
        out_specs=P("ch", ROW, None),
        check_vma=False,
    )
```

```python
import jax
import jax.numpy as jnp
from jax import lax
from jax.experimental import pallas as pl
from jax.experimental.pallas import tpu as pltpu
from jax.sharding import Mesh, PartitionSpec as P

epsilon = 1e-05
bf16 = jnp.bfloat16
f32 = jnp.float32
ROW = ("x", "z", "yh")
ALL = ("x", "z", "yh", "ch")
FIRST_Z = 8
COLUMNS = [
    [((x * 16 + (z + FIRST_Z) % 16) * 2 + yh) * 4 + q for z in range(16) for q in range(4)]
    for x in range(4)
    for yh in range(2)
]
PLANES = [
    [((d // 8 * 16 + z) * 2 + d // 4 % 2) * 4 + d % 4 for d in (p ^ 20 for p in range(32))] for z in range(16)
]
VMEM = pl.BlockSpec(memory_space=pltpu.VMEM)
HBM = pl.BlockSpec(memory_space=pltpu.HBM)


def call(kernel, outs, ins, scratch=(), flops=100_000_000):
    moved = sum(a.size * a.dtype.itemsize for a in ins)
    return pl.pallas_call(
        kernel,
        out_shape=[jax.ShapeDtypeStruct(s, d) for s, d in outs],
        in_specs=[VMEM] * len(ins),
        out_specs=[VMEM] * len(outs),
        scratch_shapes=[pltpu.VMEM(s, f32) for s in scratch],
        compiler_params=pltpu.CompilerParams(vmem_limit_bytes=32 * 1024 * 1024),
        cost_estimate=pl.CostEstimate(flops=flops, bytes_accessed=moved, transcendentals=0),
    )(*ins)


def nt(a, b):
    return lax.dot_general(a, b, (((1,), (1,)), ((), ())), preferred_element_type=f32)


def sigmoid(v):
    return 0.5 * jnp.tanh(0.5 * v) + 0.5


def norm(v, gain, bias):
    mean = jnp.mean(v, axis=0, keepdims=True)
    var = jnp.mean(v * v, axis=0, keepdims=True) - mean * mean
    return ((v - mean) * lax.rsqrt(var + epsilon) * gain + bias).astype(bf16)


def lanes(pieces):
    return jnp.concatenate(pieces, axis=1)


def permutation(k_dim=0):
    k = lax.broadcasted_iota(jnp.int32, (128, 128), k_dim)
    p = lax.broadcasted_iota(jnp.int32, (128, 128), 1 - k_dim)
    place = (k & 96) | ((k & 1) << 4) | ((k & 31) >> 1)
    return (place == p).astype(f32).astype(bf16)


def spread_kernel(x_ref, out_ref, tile, sems):
    t = jnp.dot(x_ref[...], permutation(), preferred_element_type=f32)
    for q in range(4):
        piece = lanes([t[c * 8 : c * 8 + 8, q * 32 : q * 32 + 32] for c in range(4)])
        tile[q] = piece.astype(bf16)
    copies = [pltpu.make_async_copy(tile, out_ref.at[z * 4 : z * 4 + 4], sems.at[z]) for z in range(16)]
    for c in copies:
        c.start()
    for c in copies:
        c.wait()


def spread(x):
    return pl.pallas_call(
        spread_kernel,
        out_shape=jax.ShapeDtypeStruct((64, 8, 128), bf16),
        in_specs=[VMEM],
        out_specs=HBM,
        scratch_shapes=[pltpu.VMEM((4, 8, 128), bf16), pltpu.SemaphoreType.DMA((16,))],
        compiler_params=pltpu.CompilerParams(vmem_limit_bytes=32 * 1024 * 1024),
    )(x)


def prepare_kernel(
    mask_ref, chain_ref, gain_ref, bias_ref, pb_ref, og_ref, ob_ref, wp_ref, wg_ref, wo_ref,
    packed_ref, gains_ref, pm_ref, same_ref, marks, inner, outer, sems,
):
    places = [
        (wp_ref, packed_ref.at[0:256]),
        (wg_ref, packed_ref.at[256:320]),
        (wo_ref, packed_ref.at[320:384]),
        (mask_ref, marks.at[0:1]),
        (chain_ref, marks.at[1:2]),
        (gain_ref, inner.at[0:2]),
        (bias_ref, inner.at[2:4]),
        (og_ref, outer.at[0]),
        (ob_ref, outer.at[1]),
        (pb_ref, outer.at[2]),
    ]
    copies = [pltpu.make_async_copy(a, b, sems.at[i]) for i, (a, b) in enumerate(places)]
    for c in copies[3:] + copies[:3]:
        c.start()
    ix, iyh, q = (lax.axis_index(a) for a in ("x", "yh", "ch"))
    place = lax.broadcasted_iota(jnp.int32, (128, 512), 0)
    pair = lax.broadcasted_iota(jnp.int32, (128, 512), 1)
    rows = place == (ix * 32 + iyh) + ((pair >> 5) << 1)
    columns = place == q * 32 + (((pair & 15) << 1) | ((pair >> 4) & 1))
    rows, columns = (v.astype(f32).astype(bf16) for v in (rows, columns))
    for c in copies[3:]:
        c.wait()
    m = marks[0:2, :].astype(f32)
    m = jnp.concatenate([m, jnp.zeros((6, 128), f32)], axis=0).astype(bf16)
    r = jnp.dot(m, rows, preferred_element_type=f32)
    c = jnp.dot(m, columns, preferred_element_type=f32)
    pm_ref[...] = r[0:1] * c[0:1]
    same_ref[...] = (r[1:2] == c[1:2]).astype(f32)
    g = jnp.concatenate([inner[0:4, :], jnp.zeros((124, 128), f32)], axis=0)
    gains_ref[...] = g.T[:, 0:8]
    v = jnp.concatenate([outer[i] for i in range(3)], axis=0)
    hi = v.astype(bf16).astype(f32)
    mid = (v - hi).astype(bf16).astype(f32)
    low = v - hi - mid
    v = jnp.concatenate([hi, mid, low, jnp.zeros((110, 32), f32)], axis=0)
    v = lanes([v, jnp.zeros((128, 96), f32)])
    packed_ref[384:416, :] = v.T[0:32].astype(bf16)
    for c in copies[:3]:
        c.wait()


def prepare(*args):
    return pl.pallas_call(
        prepare_kernel,
        out_shape=[
            jax.ShapeDtypeStruct((416, 128), bf16),
            jax.ShapeDtypeStruct((128, 8), f32),
            jax.ShapeDtypeStruct((1, 512), f32),
            jax.ShapeDtypeStruct((1, 512), f32),
        ],
        in_specs=[HBM] * 10,
        out_specs=[VMEM] * 4,
        scratch_shapes=[
            pltpu.VMEM((2, 128), jnp.int32),
            pltpu.VMEM((4, 128), f32),
            pltpu.VMEM((3, 2, 32), f32),
            pltpu.SemaphoreType.DMA((10,)),
        ],
        compiler_params=pltpu.CompilerParams(vmem_limit_bytes=32 * 1024 * 1024),
    )(*args)


def arrange_kernel(w_ref, cols_ref, wo_ref, own_ref, back_ref, scr):
    v = jnp.concatenate([w_ref[q, 384:416, :].astype(f32) for q in range(4)], axis=0)
    cols_ref[...] = v[:, 0:8] + v[:, 6:14] + v[:, 12:20]
    for u in range(2):
        w = jnp.concatenate([w_ref[q, 320 + u * 32 : 352 + u * 32, :] for q in range(4)], axis=0)
        w = w.astype(f32).T
        if u == 0:
            wo_ref[...] = w.astype(bf16)
        else:
            scr[...] = w
    own = pl.multiple_of(lax.axis_index("ch") * 32, 32)
    own_ref[...] = scr[pl.ds(own, 32), :].astype(bf16)
    back_ref[...] = permutation(1)


def project(n, w_ref, u, pm):
    sides = ([], [])
    for q in range(4):
        w = w_ref[q, u * 128 : u * 128 + 128, :]
        p = jnp.dot(w, n, preferred_element_type=f32)
        sides[0].append(sigmoid(p[0:32]) * p[32:64] * pm)
        sides[1].append(sigmoid(p[64:96]) * p[96:128] * pm)
    return sides


def slabs(v):
    return [lanes([a[:, z * 32 : z * 32 + 32] for a in v]) for z in range(16)]


def gates(n, w_ref, u, cols, same):
    w = jnp.concatenate([w_ref[q, 256 + u * 32 : 288 + u * 32, :] for q in range(4)], axis=0)
    return sigmoid(jnp.dot(w, n, preferred_element_type=f32) + cols * same)


def first_kernel(got_ref, gain_ref, cols_ref, w_ref, pm_ref, same_ref, out_ref, z_ref, gate_ref):
    rows = []
    for q in range(4):
        for c in range(4):
            pieces = [
                got_ref[(z - FIRST_Z) % 16 * 4 + q].astype(f32)[:, c * 32 : c * 32 + 32] for z in range(16)
            ]
            rows.append(lanes(pieces))
    z0 = jnp.concatenate(rows, axis=0)
    z_ref[...] = z0
    n = norm(z0, gain_ref[:, 0:1], gain_ref[:, 2:3])
    gate_ref[...] = gates(n, w_ref, 0, cols_ref[:, 4:5], same_ref[...])
    for s, v in enumerate(project(n, w_ref, 0, pm_ref[...])):
        v = jnp.swapaxes(jnp.stack(slabs(v), axis=0), 0, 1)
        out_ref[:, s * 16 : s * 16 + 16, :] = v.astype(bf16)


def outgoing_kernel(got_ref, out_ref):
    row = lax.broadcasted_iota(jnp.int32, (128, 512), 0) >> 5
    lane = (lax.broadcasted_iota(jnp.int32, (128, 512), 1) >> 5) & 3
    same = row == lane
    left, right = [], []
    for q in range(4):
        left.append(jnp.concatenate([got_ref[a * 4 + q ^ 20, 0:16, :] for a in range(8)], axis=0))
        right.append(jnp.concatenate([got_ref[a * 4 + q ^ 20, 16:32, :] for a in range(8)], axis=0))
    left, right = lanes(left), lanes(right)
    for q in range(4):
        part = right[q * 32 : q * 32 + 32].astype(f32)
        block = jnp.where(same, jnp.concatenate([part] * 4, axis=0), 0.0).astype(bf16)
        x = nt(left, block).astype(bf16)
        for b in range(8):
            out_ref[b * 4 + q ^ 20] = x[b * 16 : b * 16 + 16]


def middle_kernel(got_ref, z_ref, gate_ref, gain_ref, cols_ref, wo_ref, w_ref, pm_ref, out_ref, z1_ref, n1_ref):
    x = jnp.swapaxes(got_ref[...].astype(f32), 0, 1)
    x0 = jnp.concatenate(
        [lanes([x[z][:, d * 32 : d * 32 + 32] for z in range(16)]) for d in range(4)], axis=0
    )
    xn = norm(x0, cols_ref[:, 0:1], cols_ref[:, 2:3])
    y = jnp.dot(wo_ref[...], xn, preferred_element_type=f32)
    z1 = (z_ref[...] + gate_ref[...] * y).astype(bf16)
    z1_ref[...] = z1
    n1 = norm(z1.astype(f32), gain_ref[:, 1:2], gain_ref[:, 3:4])
    n1_ref[...] = n1
    left, right = project(n1, w_ref, 1, pm_ref[...])
    lane = lax.broadcasted_iota(jnp.int32, (512, 128), 0)
    col = lax.broadcasted_iota(jnp.int32, (512, 128), 1)
    want = ((col & 15) << 5) | (((col >> 4) & 1) << 4) | lax.axis_index("z")
    pick = ((lane == want) & (col < 32)).astype(f32).astype(bf16)
    left = lanes([jnp.dot(v.astype(bf16), pick, preferred_element_type=f32)[:, 0:32] for v in left])
    v = jnp.swapaxes(jnp.stack(slabs(right) + [left] * 8, axis=0), 0, 1)
    first = lax.broadcasted_iota(jnp.int32, (8, 128), 0) == 0
    for g in range(16):
        marks = jnp.where(first, v[g, 16:24], v[16 + g, 16:24]).astype(bf16)
        for yh in range(2):
            at = (g // 4 * 8 + yh * 4 + g % 4) ^ 20
            out_ref[at, 0:16, :] = v[g, 0:16].astype(bf16)
            out_ref[at, 16:32, :] = v[16 + g, 0:16].astype(bf16)
            out_ref[at, 32:40, :] = marks


def incoming_kernel(got_ref, z1_ref, n1_ref, cols_ref, w_ref, same_ref, out_ref):
    here = lax.axis_index("z")
    right = [
        lanes(
            [
                jnp.concatenate([got_ref[a * 4 + q ^ 20, h * 16 : h * 16 + 16, :] for a in range(8)], axis=0)
                for h in range(2)
            ]
        )
        for q in range(4)
    ]
    row = lax.broadcasted_iota(jnp.int32, (32, 128), 0)
    lane = lax.broadcasted_iota(jnp.int32, (32, 128), 1)
    wanted = ((row >> 3) == (lane >> 5)) & (((lane >> 4) & 1) == lax.axis_index("yh"))
    parts = []
    for a in range(8):
        tiles = [got_ref[a * 4 + x ^ 20, 32:40, :].astype(f32) for x in range(4)]
        rows = jnp.concatenate([t[h : h + 1] for h in range(2) for t in tiles], axis=0)
        parts.append(jnp.where(wanted, jnp.concatenate([rows] * 4, axis=0), 0.0).astype(bf16))
    source = lax.broadcasted_iota(jnp.int32, (1024, 128), 0)
    target = lax.broadcasted_iota(jnp.int32, (1024, 128), 1)
    place = ((source >> 7) << 4) | (source & 15)
    place = (place == target).astype(f32).astype(bf16)
    mine = jnp.dot(lanes(parts), place, preferred_element_type=f32).astype(bf16)
    prods = [jnp.dot(mine, r, preferred_element_type=f32) for r in right]
    upper = lax.broadcasted_iota(jnp.int32, (8, 128), 0) < 4
    xs = []
    for d in range(4):
        h0, h1 = (
            lanes([p[d * 8 : d * 8 + 8, h * 128 + d * 32 : h * 128 + d * 32 + 32] for p in prods])
            for h in range(2)
        )
        xs.append(jnp.where(upper, h0, h1))
    x = jnp.swapaxes(jnp.stack(xs + xs, axis=0), 0, 1)
    x = [jnp.where(upper, x[i], x[4 + i]).astype(bf16) for i in range(4)]
    lane = lax.broadcasted_iota(jnp.int32, (512, 128), 0)
    col = lax.broadcasted_iota(jnp.int32, (512, 128), 1)
    pick = ((lane == here * 32 + col) & (col < 32)).astype(f32).astype(bf16)
    z1 = jnp.dot(z1_ref[...], pick, preferred_element_type=f32)
    n1 = jnp.dot(n1_ref[...], pick, preferred_element_type=f32).astype(bf16)
    same = jnp.dot(
        jnp.broadcast_to(same_ref[...], (8, 512)).astype(bf16), pick, preferred_element_type=f32
    )[0:1]
    gate = gates(n1, w_ref, 1, cols_ref[:, 5:6], same)
    for q in range(4):
        zq, gq = (
            lanes([v[q * 32 + c * 8 : q * 32 + c * 8 + 8, 0:32] for c in range(4)]).astype(bf16)
            for v in (z1, gate)
        )
        for a in range(4):
            out_ref[a * 4 + q, 0:8, :] = x[a]
            out_ref[a * 4 + q, 8:16, :] = zq
            out_ref[a * 4 + q, 16:24, :] = gq


def last_kernel(got_ref, cols_ref, own_ref, back_ref, out_ref):
    x = jnp.swapaxes(got_ref[:, 0:8, :].astype(f32), 0, 1)
    x1 = jnp.concatenate([x[h * 4 + d] for d in range(4) for h in range(2)], axis=0)
    xn = norm(x1, cols_ref[:, 1:2], cols_ref[:, 3:4])
    y = jnp.dot(own_ref[...], xn, preferred_element_type=f32)
    home = lax.axis_index("x") * 4
    own = [got_ref[home + s].astype(f32) for s in range(4)]
    z1, gate = (
        jnp.concatenate(
            [lanes([o[r : r + 8, c * 32 : c * 32 + 32] for o in own]) for c in range(4)], axis=0
        )
        for r in (8, 16)
    )
    out = (z1 + gate * y).astype(bf16)
    out_ref[...] = jnp.dot(out, back_ref[...], preferred_element_type=f32).astype(bf16)


def body(pair_rep, residue_mask, chain_ids, in_gain, in_bias, w_proj, w_gate, pair_bias, out_gain, out_bias, w_out):
    send = spread(pair_rep.reshape(32, 128))
    args = (
        residue_mask.reshape(1, 128),
        chain_ids.reshape(1, 128),
        in_gain,
        in_bias,
        pair_bias,
        out_gain,
        out_bias,
        w_proj.transpose(0, 2, 3, 1).reshape(256, 128),
        w_gate.transpose(0, 2, 1).reshape(64, 128),
        w_out.reshape(64, 128),
    )
    send, *args = lax.optimization_barrier((send, *args))
    got = lax.all_to_all(send, ALL, 0, 0, axis_index_groups=COLUMNS, tiled=True)
    packed, gains, pm, same = prepare(*args)
    packed = lax.all_gather(packed, "ch", axis=0)
    cols, wo, own, back = call(
        arrange_kernel,
        [((128, 8), f32), ((128, 128), bf16), ((32, 128), bf16), ((128, 128), bf16)],
        [packed],
        [(128, 128)],
        flops=1_000_000,
    )
    got, packed, gains, pm, same, cols, wo, own, back = lax.optimization_barrier(
        (got, packed, gains, pm, same, cols, wo, own, back)
    )
    send, z0, gate = call(
        first_kernel,
        [((32, 32, 128), bf16), ((128, 512), f32), ((128, 512), f32)],
        [got, gains, cols, packed, pm, same],
    )
    got = lax.all_to_all(send, ALL, 0, 0, axis_index_groups=PLANES, tiled=True)
    (send,) = call(outgoing_kernel, [((32, 16, 128), bf16)], [got])
    got = lax.all_to_all(send, ALL, 0, 0, axis_index_groups=PLANES, tiled=True)
    send, z1, n1 = call(
        middle_kernel,
        [((32, 40, 128), bf16), ((128, 512), bf16), ((128, 512), bf16)],
        [got, z0, gate, gains, cols, wo, packed, pm],
    )
    got = lax.all_to_all(send, ALL, 0, 0, axis_index_groups=PLANES, tiled=True)
    (send,) = call(incoming_kernel, [((16, 24, 128), bf16)], [got, z1, n1, cols, packed, same])
    got = lax.all_to_all(send, ("x", "ch"), 0, 0, tiled=True)
    (out,) = call(last_kernel, [((32, 128), bf16)], [got, cols, own, back])
    return out.reshape(32, 1, 128)


def solution(mesh):
    fine = Mesh(mesh.devices.reshape(4, 16, 2, 4), ("x", "z", "yh", "ch"))
    return jax.shard_map(
        body,
        mesh=fine,
        in_specs=(
            P("ch", ROW, None),
            P(),
            P(),
            P(),
            P(),
            P(None, None, None, "ch"),
            P(None, None, "ch"),
            P(None, "ch"),
            P(None, "ch"),
            P(None, "ch"),
            P(None, "ch", None),
        ),
        out_specs=P("ch", ROW, None),
        check_vma=False,
    )
```

```python
import jax
import jax.numpy as jnp
from jax import lax
from jax.experimental import pallas as pl
from jax.experimental.pallas import tpu as pltpu
from jax.sharding import Mesh, PartitionSpec as P

epsilon = 1e-05
bf16 = jnp.bfloat16
f32 = jnp.float32
ROW = ("x", "z", "yh")
ALL = ("x", "z", "yh", "ch")
FIRST_Z = 8
COLUMNS = [
    [((x * 16 + (z + FIRST_Z) % 16) * 2 + yh) * 4 + q for z in range(16) for q in range(4)]
    for x in range(4)
    for yh in range(2)
]
PLANES = [
    [((d // 8 * 16 + z) * 2 + d // 4 % 2) * 4 + d % 4 for d in (p ^ 20 for p in range(32))] for z in range(16)
]
LINES = [
    [((d // 4 * 16 + z) * 2 + yh) * 4 + d % 4 for d in (p ^ 8 for p in range(16))]
    for z in range(16)
    for yh in range(2)
]
VMEM = pl.BlockSpec(memory_space=pltpu.VMEM)
HBM = pl.BlockSpec(memory_space=pltpu.HBM)


def call(kernel, outs, ins, scratch=(), flops=100_000_000):
    moved = sum(a.size * a.dtype.itemsize for a in ins)
    return pl.pallas_call(
        kernel,
        out_shape=[jax.ShapeDtypeStruct(s, d) for s, d in outs],
        in_specs=[VMEM] * len(ins),
        out_specs=[VMEM] * len(outs),
        scratch_shapes=[pltpu.VMEM(s, f32) for s in scratch],
        compiler_params=pltpu.CompilerParams(vmem_limit_bytes=32 * 1024 * 1024),
        cost_estimate=pl.CostEstimate(flops=flops, bytes_accessed=moved, transcendentals=0),
    )(*ins)


def nt(a, b):
    return lax.dot_general(a, b, (((1,), (1,)), ((), ())), preferred_element_type=f32)


def sigmoid(v):
    return 0.5 * jnp.tanh(0.5 * v) + 0.5


def norm(v, gain, bias):
    mean = jnp.mean(v, axis=0, keepdims=True)
    var = jnp.mean(v * v, axis=0, keepdims=True) - mean * mean
    return ((v - mean) * lax.rsqrt(var + epsilon) * gain + bias).astype(bf16)


def lanes(pieces):
    return jnp.concatenate(pieces, axis=1)


def permutation(k_dim=0):
    k = lax.broadcasted_iota(jnp.int32, (128, 128), k_dim)
    p = lax.broadcasted_iota(jnp.int32, (128, 128), 1 - k_dim)
    place = (k & 96) | ((k & 1) << 4) | ((k & 31) >> 1)
    return (place == p).astype(f32).astype(bf16)


def spread_kernel(x_ref, out_ref, tile, sems):
    t = jnp.dot(x_ref[...], permutation(), preferred_element_type=f32)
    for q in range(4):
        piece = lanes([t[c * 8 : c * 8 + 8, q * 32 : q * 32 + 32] for c in range(4)])
        tile[q] = piece.astype(bf16)
    copies = [pltpu.make_async_copy(tile, out_ref.at[z * 4 : z * 4 + 4], sems.at[z]) for z in range(16)]
    for c in copies:
        c.start()
    for c in copies:
        c.wait()


def spread(x):
    return pl.pallas_call(
        spread_kernel,
        out_shape=jax.ShapeDtypeStruct((64, 8, 128), bf16),
        in_specs=[VMEM],
        out_specs=HBM,
        scratch_shapes=[pltpu.VMEM((4, 8, 128), bf16), pltpu.SemaphoreType.DMA((16,))],
        compiler_params=pltpu.CompilerParams(vmem_limit_bytes=32 * 1024 * 1024),
    )(x)


def prepare_kernel(
    mask_ref, chain_ref, gain_ref, bias_ref, pb_ref, og_ref, ob_ref, wp_ref, wg_ref, wo_ref,
    packed_ref, gains_ref, pm_ref, same_ref, marks, inner, outer, sems,
):
    places = [
        (wp_ref, packed_ref.at[0:256]),
        (wg_ref, packed_ref.at[256:320]),
        (wo_ref, packed_ref.at[320:384]),
        (mask_ref, marks.at[0:1]),
        (chain_ref, marks.at[1:2]),
        (gain_ref, inner.at[0:2]),
        (bias_ref, inner.at[2:4]),
        (og_ref, outer.at[0]),
        (ob_ref, outer.at[1]),
        (pb_ref, outer.at[2]),
    ]
    copies = [pltpu.make_async_copy(a, b, sems.at[i]) for i, (a, b) in enumerate(places)]
    for c in copies[3:] + copies[:3]:
        c.start()
    ix, iyh, q = (lax.axis_index(a) for a in ("x", "yh", "ch"))
    place = lax.broadcasted_iota(jnp.int32, (128, 512), 0)
    pair = lax.broadcasted_iota(jnp.int32, (128, 512), 1)
    rows = place == (ix * 32 + iyh) + ((pair >> 5) << 1)
    columns = place == q * 32 + (((pair & 15) << 1) | ((pair >> 4) & 1))
    rows, columns = (v.astype(f32).astype(bf16) for v in (rows, columns))
    for c in copies[3:]:
        c.wait()
    m = marks[0:2, :].astype(f32)
    m = jnp.concatenate([m, jnp.zeros((6, 128), f32)], axis=0).astype(bf16)
    r = jnp.dot(m, rows, preferred_element_type=f32)
    c = jnp.dot(m, columns, preferred_element_type=f32)
    pm_ref[...] = r[0:1] * c[0:1]
    same_ref[...] = (r[1:2] == c[1:2]).astype(f32)
    g = jnp.concatenate([inner[0:4, :], jnp.zeros((124, 128), f32)], axis=0)
    gains_ref[...] = g.T[:, 0:8]
    v = jnp.concatenate([outer[i] for i in range(3)], axis=0)
    hi = v.astype(bf16).astype(f32)
    mid = (v - hi).astype(bf16).astype(f32)
    low = v - hi - mid
    v = jnp.concatenate([hi, mid, low, jnp.zeros((110, 32), f32)], axis=0)
    v = lanes([v, jnp.zeros((128, 96), f32)])
    packed_ref[384:416, :] = v.T[0:32].astype(bf16)
    for c in copies[:3]:
        c.wait()


def prepare(*args):
    return pl.pallas_call(
        prepare_kernel,
        out_shape=[
            jax.ShapeDtypeStruct((416, 128), bf16),
            jax.ShapeDtypeStruct((128, 8), f32),
            jax.ShapeDtypeStruct((1, 512), f32),
            jax.ShapeDtypeStruct((1, 512), f32),
        ],
        in_specs=[HBM] * 10,
        out_specs=[VMEM] * 4,
        scratch_shapes=[
            pltpu.VMEM((2, 128), jnp.int32),
            pltpu.VMEM((4, 128), f32),
            pltpu.VMEM((3, 2, 32), f32),
            pltpu.SemaphoreType.DMA((10,)),
        ],
        compiler_params=pltpu.CompilerParams(vmem_limit_bytes=32 * 1024 * 1024),
    )(*args)


def arrange_kernel(w_ref, cols_ref, wo_ref, own_ref, back_ref, scr):
    v = jnp.concatenate([w_ref[q, 384:416, :].astype(f32) for q in range(4)], axis=0)
    cols_ref[...] = v[:, 0:8] + v[:, 6:14] + v[:, 12:20]
    for u in range(2):
        w = jnp.concatenate([w_ref[q, 320 + u * 32 : 352 + u * 32, :] for q in range(4)], axis=0)
        w = w.astype(f32).T
        if u == 0:
            wo_ref[...] = w.astype(bf16)
        else:
            scr[...] = w
    own = pl.multiple_of(lax.axis_index("ch") * 32, 32)
    own_ref[...] = scr[pl.ds(own, 32), :].astype(bf16)
    back_ref[...] = permutation(1)


def project(n, w_ref, u, pm):
    sides = ([], [])
    for q in range(4):
        w = w_ref[q, u * 128 : u * 128 + 128, :]
        p = jnp.dot(w, n, preferred_element_type=f32)
        sides[0].append(sigmoid(p[0:32]) * p[32:64] * pm)
        sides[1].append(sigmoid(p[64:96]) * p[96:128] * pm)
    return sides


def slabs(v):
    return [lanes([a[:, z * 32 : z * 32 + 32] for a in v]) for z in range(16)]


def gates(n, w_ref, u, cols, same):
    w = jnp.concatenate([w_ref[q, 256 + u * 32 : 288 + u * 32, :] for q in range(4)], axis=0)
    return sigmoid(jnp.dot(w, n, preferred_element_type=f32) + cols * same)


def first_kernel(got_ref, gain_ref, cols_ref, w_ref, pm_ref, same_ref, out_ref, z_ref, gate_ref):
    rows = []
    for q in range(4):
        for c in range(4):
            pieces = [
                got_ref[(z - FIRST_Z) % 16 * 4 + q].astype(f32)[:, c * 32 : c * 32 + 32] for z in range(16)
            ]
            rows.append(lanes(pieces))
    z0 = jnp.concatenate(rows, axis=0)
    z_ref[...] = z0
    n = norm(z0, gain_ref[:, 0:1], gain_ref[:, 2:3])
    gate_ref[...] = gates(n, w_ref, 0, cols_ref[:, 4:5], same_ref[...])
    for s, v in enumerate(project(n, w_ref, 0, pm_ref[...])):
        v = jnp.swapaxes(jnp.stack(slabs(v), axis=0), 0, 1)
        out_ref[:, s * 16 : s * 16 + 16, :] = v.astype(bf16)


def outgoing_kernel(got_ref, out_ref):
    row = lax.broadcasted_iota(jnp.int32, (128, 512), 0) >> 5
    lane = (lax.broadcasted_iota(jnp.int32, (128, 512), 1) >> 5) & 3
    same = row == lane
    left, right = [], []
    for q in range(4):
        left.append(jnp.concatenate([got_ref[a * 4 + q ^ 20, 0:16, :] for a in range(8)], axis=0))
        right.append(jnp.concatenate([got_ref[a * 4 + q ^ 20, 16:32, :] for a in range(8)], axis=0))
    left, right = lanes(left), lanes(right)
    for q in range(4):
        part = right[q * 32 : q * 32 + 32].astype(f32)
        block = jnp.where(same, jnp.concatenate([part] * 4, axis=0), 0.0).astype(bf16)
        x = nt(left, block).astype(bf16)
        for b in range(8):
            out_ref[b * 4 + q ^ 20] = x[b * 16 : b * 16 + 16]


def middle_kernel(got_ref, z_ref, gate_ref, gain_ref, cols_ref, wo_ref, w_ref, pm_ref, out_ref, z1_ref, n1_ref):
    x = jnp.swapaxes(got_ref[...].astype(f32), 0, 1)
    x0 = jnp.concatenate(
        [lanes([x[z][:, d * 32 : d * 32 + 32] for z in range(16)]) for d in range(4)], axis=0
    )
    xn = norm(x0, cols_ref[:, 0:1], cols_ref[:, 2:3])
    y = jnp.dot(wo_ref[...], xn, preferred_element_type=f32)
    z1 = (z_ref[...] + gate_ref[...] * y).astype(bf16)
    z1_ref[...] = z1
    n1 = norm(z1.astype(f32), gain_ref[:, 1:2], gain_ref[:, 3:4])
    n1_ref[...] = n1
    left, right = project(n1, w_ref, 1, pm_ref[...])
    lane = lax.broadcasted_iota(jnp.int32, (512, 128), 0)
    col = lax.broadcasted_iota(jnp.int32, (512, 128), 1)
    want = ((col & 15) << 5) | (((col >> 4) & 1) << 4) | lax.axis_index("z")
    pick = ((lane == want) & (col < 32)).astype(f32).astype(bf16)
    left = lanes([jnp.dot(v.astype(bf16), pick, preferred_element_type=f32)[:, 0:32] for v in left])
    v = jnp.swapaxes(jnp.stack(slabs(right) + [left] * 8, axis=0), 0, 1)
    first = lax.broadcasted_iota(jnp.int32, (8, 128), 0) == 0
    for g in range(16):
        marks = jnp.where(first, v[g, 16:24], v[16 + g, 16:24]).astype(bf16)
        for yh in range(2):
            at = (g // 4 * 8 + yh * 4 + g % 4) ^ 20
            out_ref[at, 0:16, :] = v[g, 0:16].astype(bf16)
            out_ref[at, 16:32, :] = v[16 + g, 0:16].astype(bf16)
            out_ref[at, 32:40, :] = marks


def incoming_kernel(got_ref, z1_ref, n1_ref, cols_ref, w_ref, same_ref, out_ref):
    here = lax.axis_index("z")
    right = [
        lanes(
            [
                jnp.concatenate([got_ref[a * 4 + q ^ 20, h * 16 : h * 16 + 16, :] for a in range(8)], axis=0)
                for h in range(2)
            ]
        )
        for q in range(4)
    ]
    row = lax.broadcasted_iota(jnp.int32, (32, 128), 0)
    lane = lax.broadcasted_iota(jnp.int32, (32, 128), 1)
    wanted = ((row >> 3) == (lane >> 5)) & (((lane >> 4) & 1) == lax.axis_index("yh"))
    parts = []
    for a in range(8):
        tiles = [got_ref[a * 4 + x ^ 20, 32:40, :].astype(f32) for x in range(4)]
        rows = jnp.concatenate([t[h : h + 1] for h in range(2) for t in tiles], axis=0)
        parts.append(jnp.where(wanted, jnp.concatenate([rows] * 4, axis=0), 0.0).astype(bf16))
    source = lax.broadcasted_iota(jnp.int32, (1024, 128), 0)
    target = lax.broadcasted_iota(jnp.int32, (1024, 128), 1)
    place = ((source >> 7) << 4) | (source & 15)
    place = (place == target).astype(f32).astype(bf16)
    mine = jnp.dot(lanes(parts), place, preferred_element_type=f32).astype(bf16)
    prods = [jnp.dot(mine, r, preferred_element_type=f32) for r in right]
    upper = lax.broadcasted_iota(jnp.int32, (8, 128), 0) < 4
    xs = []
    for d in range(4):
        h0, h1 = (
            lanes([p[d * 8 : d * 8 + 8, h * 128 + d * 32 : h * 128 + d * 32 + 32] for p in prods])
            for h in range(2)
        )
        xs.append(jnp.where(upper, h0, h1))
    x = jnp.swapaxes(jnp.stack(xs + xs, axis=0), 0, 1)
    x = [jnp.where(upper, x[i], x[4 + i]).astype(bf16) for i in range(4)]
    lane = lax.broadcasted_iota(jnp.int32, (512, 128), 0)
    col = lax.broadcasted_iota(jnp.int32, (512, 128), 1)
    pick = ((lane == here * 32 + col) & (col < 32)).astype(f32).astype(bf16)
    z1 = jnp.dot(z1_ref[...], pick, preferred_element_type=f32)
    n1 = jnp.dot(n1_ref[...], pick, preferred_element_type=f32).astype(bf16)
    same = jnp.dot(
        jnp.broadcast_to(same_ref[...], (8, 512)).astype(bf16), pick, preferred_element_type=f32
    )[0:1]
    gate = gates(n1, w_ref, 1, cols_ref[:, 5:6], same)
    for q in range(4):
        zq, gq = (
            lanes([v[q * 32 + c * 8 : q * 32 + c * 8 + 8, 0:32] for c in range(4)]).astype(bf16)
            for v in (z1, gate)
        )
        for a in range(4):
            out_ref[a * 4 + q ^ 8, 0:8, :] = x[a]
            out_ref[a * 4 + q ^ 8, 8:16, :] = zq
            out_ref[a * 4 + q ^ 8, 16:24, :] = gq


def last_kernel(got_ref, cols_ref, own_ref, back_ref, out_ref):
    x = jnp.swapaxes(got_ref[:, 0:8, :].astype(f32), 0, 1)
    x1 = jnp.concatenate([x[h * 4 + d, g : g + 8] for d in range(4) for h in range(2) for g in (8, 0)], axis=0)
    xn = norm(x1, cols_ref[:, 1:2], cols_ref[:, 3:4])
    y = jnp.dot(own_ref[...], xn, preferred_element_type=f32)
    home = (lax.axis_index("x") ^ 2) * 4
    own = [got_ref[home + s].astype(f32) for s in range(4)]
    z1, gate = (
        jnp.concatenate(
            [lanes([o[r : r + 8, c * 32 : c * 32 + 32] for o in own]) for c in range(4)], axis=0
        )
        for r in (8, 16)
    )
    out = (z1 + gate * y).astype(bf16)
    out_ref[...] = jnp.dot(out, back_ref[...], preferred_element_type=f32).astype(bf16)


def body(pair_rep, residue_mask, chain_ids, in_gain, in_bias, w_proj, w_gate, pair_bias, out_gain, out_bias, w_out):
    send = spread(pair_rep.reshape(32, 128))
    args = (
        residue_mask.reshape(1, 128),
        chain_ids.reshape(1, 128),
        in_gain,
        in_bias,
        pair_bias,
        out_gain,
        out_bias,
        w_proj.transpose(0, 2, 3, 1).reshape(256, 128),
        w_gate.transpose(0, 2, 1).reshape(64, 128),
        w_out.reshape(64, 128),
    )
    send, *args = lax.optimization_barrier((send, *args))
    got = lax.all_to_all(send, ALL, 0, 0, axis_index_groups=COLUMNS, tiled=True)
    packed, gains, pm, same = prepare(*args)
    packed = lax.all_gather(packed, "ch", axis=0)
    cols, wo, own, back = call(
        arrange_kernel,
        [((128, 8), f32), ((128, 128), bf16), ((32, 128), bf16), ((128, 128), bf16)],
        [packed],
        [(128, 128)],
        flops=1_000_000,
    )
    got, packed, gains, pm, same, cols, wo, own, back = lax.optimization_barrier(
        (got, packed, gains, pm, same, cols, wo, own, back)
    )
    send, z0, gate = call(
        first_kernel,
        [((32, 32, 128), bf16), ((128, 512), f32), ((128, 512), f32)],
        [got, gains, cols, packed, pm, same],
    )
    got = lax.all_to_all(send, ALL, 0, 0, axis_index_groups=PLANES, tiled=True)
    (send,) = call(outgoing_kernel, [((32, 16, 128), bf16)], [got])
    got = lax.all_to_all(send, ALL, 0, 0, axis_index_groups=PLANES, tiled=True)
    send, z1, n1 = call(
        middle_kernel,
        [((32, 40, 128), bf16), ((128, 512), bf16), ((128, 512), bf16)],
        [got, z0, gate, gains, cols, wo, packed, pm],
    )
    got = lax.all_to_all(send, ALL, 0, 0, axis_index_groups=PLANES, tiled=True)
    (send,) = call(incoming_kernel, [((16, 24, 128), bf16)], [got, z1, n1, cols, packed, same])
    got = lax.all_to_all(send, ALL, 0, 0, axis_index_groups=LINES, tiled=True)
    (out,) = call(last_kernel, [((32, 128), bf16)], [got, cols, own, back])
    return out.reshape(32, 1, 128)


def solution(mesh):
    fine = Mesh(mesh.devices.reshape(4, 16, 2, 4), ("x", "z", "yh", "ch"))
    return jax.shard_map(
        body,
        mesh=fine,
        in_specs=(
            P("ch", ROW, None),
            P(),
            P(),
            P(),
            P(),
            P(None, None, None, "ch"),
            P(None, None, "ch"),
            P(None, "ch"),
            P(None, "ch"),
            P(None, "ch"),
            P(None, "ch", None),
        ),
        out_specs=P("ch", ROW, None),
        check_vma=False,
    )
```
